256 devices in a mesh: sail: 32 (over y, z), cable: 8 (over x, core).
Axes of the slice: x: 4, y: 4, z: 8, core: 2. Of those that a mesh axis runs over, the one named last changes fastest.
Arguments:
- traces: bfloat16 [524288, 512], P(('sail', 'cable')), may hold values from -6 to 6
- src_index: int32 [16384, 128], P(('sail', 'cable')), may hold values from 0 to 2175
- rcv_index: int32 [16384, 128], P(('sail', 'cable')), may hold values from 0 to 4095
- taper_index: int32 [16384, 128], P(('sail', 'cable')), may hold values from 0 to 15
- fetch_rows: int32 [8192, 128], P(('sail', 'cable')), may hold values from 0 to 2047, as said below
- line_owner: int32 [32], replicated, may hold values from 0 to 31, each once
- taper_table: float32 [16], replicated, may hold values from 0.2 to 1
Outputs:
- predicted: bfloat16 [16384, 512], P(('sail', 'cable'))
The draws below stay inside these ranges and needn't reach their ends.
Inputs may be any that keep to these rules, and one draw needn't show every extreme that they name: Each row of fetch_rows names exactly 64 distinct traces.
All inputs are finite; a program needn't handle non-finite values.
Results may differ from the reference program's by a relative error of at most 0.0084.
Values may be sent and summed in bfloat16 or wider, within the bound.
No kernel may reach another device: no remote copies, remote signals or barrier semaphores. Data moves between devices by JAX's collectives and lax.ppermute only.
A program may use at most 64 MiB of HBM per device.

```python
import math
import jax
import jax.numpy as jnp
from jax import lax

NT = 512
NF = 256
APER = 128
OUT_DEV = 64
TR_DEV = 2048
HALO = 64
CAP = 128
DISTINCT = 64
TAPERS = 16
SLOTS = 4096
TRACES = 524288
OUTS = 16384
REQS = 8192
N_SAIL = 32
N_CABLE = 8


def draw_fetch_rows(key, part):
    key = jax.random.fold_in(key, 5)
    key_order, key_extra, key_place = jax.random.split(key, 3)
    bits = jax.random.randint(key_order, (REQS, TR_DEV), 0, 2 ** 20, dtype=jnp.int32)
    order = jnp.argsort(bits * TR_DEV + jnp.arange(TR_DEV, dtype=jnp.int32)[None, :], axis=1)
    picked = order[:, :DISTINCT].astype(jnp.int32)
    extra = jax.random.randint(key_extra, (REQS, CAP - DISTINCT), 0, DISTINCT, dtype=jnp.int32)
    repeated = jnp.take_along_axis(picked, extra, axis=1)
    filled = jnp.concatenate([picked, repeated], axis=1)
    place_bits = jax.random.randint(key_place, (REQS, CAP), 0, 2 ** 20, dtype=jnp.int32)
    placing = jnp.argsort(place_bits * CAP + jnp.arange(CAP, dtype=jnp.int32)[None, :], axis=1)
    return jnp.take_along_axis(filled, placing, axis=1).astype(jnp.int32)


def set_ends(entries, key, smallest, largest):
    place = [jax.random.randint(jax.random.fold_in(key, axis), (), 0, length) for axis, length in enumerate(entries.shape)]
    main_axis = entries.shape.index(max(entries.shape))
    beside = place[:main_axis] + [(place[main_axis] + 1) % entries.shape[main_axis]] + place[main_axis + 1:]
    return entries.at[tuple(place)].set(smallest).at[tuple(beside)].set(largest)


def shard_levels(key, shape, cuts, smallest, largest):
    def one(position, blocks):
        draws = jax.random.uniform(jax.random.fold_in(jax.random.fold_in(key, 6), position), (blocks,), jnp.float32, smallest / len(cuts), largest / len(cuts))
        return jnp.repeat(jnp.exp(draws), shape[position] // blocks).reshape((-1,) + (1,) * (len(shape) - position - 1))

    level = one(*cuts[0])
    for cut in cuts[1:]:
        level = level * one(*cut)
    return level


def normal_values(key, extent, scale, bound, cuts=(), kind=jnp.bfloat16):
    gain = shard_levels(key, extent, cuts, -0.22, 0.18) if cuts else 1.0
    drawn = jax.random.normal(key, extent, jnp.float32) * scale * gain
    return jnp.minimum(jnp.maximum(drawn, -bound), bound).astype(kind)


def setup_inputs(seed: int = 0) -> dict:
    seeds = jax.random.split(jax.random.key(seed), 8)
    traces = normal_values(seeds[0], (TRACES, NT), 1.0, 6.0, ((0, 256),))
    src_index = set_ends(jax.random.randint(seeds[1], (OUTS, APER), 0, TR_DEV + 2 * HALO), jax.random.fold_in(seeds[1], 1), 0, (TR_DEV + 2 * HALO) - 1).astype(jnp.int32)
    rcv_index = set_ends(jax.random.randint(seeds[2], (OUTS, APER), 0, SLOTS), jax.random.fold_in(seeds[2], 1), 0, SLOTS - 1).astype(jnp.int32)
    taper_index = set_ends(jax.random.randint(seeds[3], (OUTS, APER), 0, TAPERS), jax.random.fold_in(seeds[3], 1), 0, TAPERS - 1).astype(jnp.int32)
    fetch_rows = draw_fetch_rows(jax.random.fold_in(seeds[7], 71), 0)
    line_owner = jax.random.permutation(seeds[5], N_SAIL).astype(jnp.int32)
    taper_table = jnp.clip(jax.random.uniform(seeds[6], (TAPERS,), jnp.float32, 0.2, 1.0), 0.2, 1.0)
    return dict(traces=traces, src_index=src_index, rcv_index=rcv_index, taper_index=taper_index, fetch_rows=fetch_rows, line_owner=line_owner, taper_table=taper_table)


def forward_table(samples):
    times = jnp.arange(samples, dtype=jnp.int32)
    freqs = jnp.arange(samples // 2, dtype=jnp.int32)
    turns = times[:, None] * freqs[None, :] % samples
    angle = turns.astype(jnp.float32) * (2.0 * math.pi / samples)
    scale = 1.0 / math.sqrt(samples)
    return (jnp.concatenate([jnp.cos(angle), -jnp.sin(angle)], axis=1) * scale).astype(jnp.bfloat16)

def synthesis_table(samples, aperture):
    freqs = jnp.arange(samples // 2, dtype=jnp.int32)
    times = jnp.arange(samples, dtype=jnp.int32)
    turns = freqs[:, None] * times[None, :] % samples
    angle = turns.astype(jnp.float32) * (2.0 * math.pi / samples)
    scale = 1.0 / math.sqrt(aperture * (samples // 2))
    return (jnp.concatenate([jnp.cos(angle), -jnp.sin(angle)], axis=0) * scale).astype(jnp.bfloat16)

def predict_block(src_rows, rcv_rows, weights):
    half = src_rows.shape[-1] // 2
    left = src_rows.astype(jnp.float32)
    right = rcv_rows.astype(jnp.float32)
    real_part = left[..., :half] * right[..., :half] - left[..., half:] * right[..., half:]
    imag_part = left[..., :half] * right[..., half:] + left[..., half:] * right[..., :half]
    scaled = weights[..., None]
    return jnp.concatenate([lax.optimization_barrier(jnp.sum(scaled * real_part, axis=1)), lax.optimization_barrier(jnp.sum(scaled * imag_part, axis=1))], axis=-1)

def reference(traces, src_index, rcv_index, taper_index, fetch_rows, line_owner, taper_table):
    spectra = jnp.dot(traces, forward_table(NT), preferred_element_type=jnp.float32).astype(jnp.bfloat16)
    synth = synthesis_table(NT, APER)
    block = min(256, OUTS)
    count = OUTS // block
    taper_ids = jnp.arange(TAPERS, dtype=jnp.int32)

    def one_block(pieces):
        out_ids, s_idx, r_idx, t_idx = pieces
        device = out_ids // OUT_DEV
        sail_i = device // N_CABLE
        cable_j = device % N_CABLE
        shift = jnp.where(s_idx < HALO, -1, jnp.where(s_idx >= TR_DEV + HALO, 1, 0)).astype(jnp.int32)
        neighbour = cable_j[:, None] + shift
        valid = (neighbour >= 0) & (neighbour < N_CABLE)
        row = s_idx - HALO - shift * TR_DEV
        src_glob = (sail_i[:, None] * N_CABLE + jnp.clip(neighbour, 0, N_CABLE - 1)) * TR_DEV + row
        src_rows = jnp.take(spectra, src_glob.astype(jnp.int32), axis=0)
        src_rows = jnp.where(valid[..., None], src_rows, jnp.zeros_like(src_rows))
        line = r_idx // CAP
        slot = r_idx % CAP
        fetched = fetch_rows[(device[:, None] * N_SAIL + line).astype(jnp.int32), slot.astype(jnp.int32)]
        rcv_glob = (line_owner[line] * N_CABLE + cable_j[:, None]) * TR_DEV + fetched
        rcv_rows = jnp.take(spectra, rcv_glob.astype(jnp.int32), axis=0)
        weights = lax.optimization_barrier(jnp.sum(jnp.where(t_idx[..., None] == taper_ids, taper_table, jnp.zeros_like(taper_table)), axis=-1))
        return predict_block(src_rows, rcv_rows, weights).astype(jnp.bfloat16)
    out_ids = jnp.arange(OUTS, dtype=jnp.int32).reshape(count, block)
    summed = lax.map(one_block, (out_ids, src_index.reshape(count, block, APER), rcv_index.reshape(count, block, APER), taper_index.reshape(count, block, APER)))
    summed = summed.reshape(OUTS, 2 * NF)
    return jnp.dot(summed, synth, preferred_element_type=jnp.float32).astype(jnp.bfloat16)
```

```python
import functools
import math

import jax
import jax.numpy as jnp
from jax import lax
from jax.experimental import pallas as pl
from jax.experimental.pallas import tpu as pltpu
from jax.sharding import PartitionSpec as P

HALO = 64
DISTINCT = 64
F32 = jnp.float32
BF16 = jnp.bfloat16


def forward_table(samples):
    times = jnp.arange(samples, dtype=jnp.int32)
    freqs = jnp.arange(samples // 2, dtype=jnp.int32)
    turns = times[:, None] * freqs[None, :] % samples
    angle = turns.astype(jnp.float32) * (2.0 * math.pi / samples)
    scale = 1.0 / math.sqrt(samples)
    return (jnp.concatenate([jnp.cos(angle), -jnp.sin(angle)], axis=1) * scale).astype(jnp.bfloat16)


def synthesis_table(samples, aperture):
    freqs = jnp.arange(samples // 2, dtype=jnp.int32)
    times = jnp.arange(samples, dtype=jnp.int32)
    turns = freqs[:, None] * times[None, :] % samples
    angle = turns.astype(jnp.float32) * (2.0 * math.pi / samples)
    scale = 1.0 / math.sqrt(aperture * (samples // 2))
    return (jnp.concatenate([jnp.cos(angle), -jnp.sin(angle)], axis=0) * scale).astype(jnp.bfloat16)


def distinct_kernel(owner_ref, rows_ref, asked_ref, place_ref):
    lines, cap = rows_ref.shape
    rows = rows_ref[...]
    sub = lax.broadcasted_iota(jnp.int32, (cap, cap), 0)
    lane = lax.broadcasted_iota(jnp.int32, (cap, cap), 1)
    pad = jnp.zeros((cap - lines, cap), jnp.int32)

    def turned(values):
        return jnp.concatenate([values, pad], axis=0).T

    columns = turned(rows)
    once = []
    for g in range(lines):
        column = columns[:, g : g + 1]
        row = rows[g : g + 1, :]
        repeats = jnp.sum(((column == row) & (sub < lane)).astype(jnp.int32), axis=0, keepdims=True)
        once.append(jnp.where(repeats == 0, row, 1 << 20))
    once_columns = turned(jnp.concatenate(once, axis=0))
    ranks = []
    for g in range(lines):
        smaller = (once_columns[:, g : g + 1] < rows[g : g + 1, :]).astype(jnp.int32)
        ranks.append(jnp.sum(smaller, axis=0, keepdims=True))
    rank_columns = turned(jnp.concatenate(ranks, axis=0))
    for g in range(lines):
        match = rank_columns[:, g : g + 1] == lane
        picked = jnp.max(jnp.where(match, columns[:, g : g + 1], 0), axis=0, keepdims=True)
        asked_ref[owner_ref[g]] = picked
        place_ref[g : g + 1, :] = ranks[g] + owner_ref[g] * DISTINCT


def quarters(block):
    return [block[:, 128 * q : 128 * (q + 1)] for q in range(4)]


def put_sources(wide_ref, start, block):
    r0, r1, i0, i1 = quarters(block)
    for j, piece in enumerate((r0, r1, i0, i1, i0, i1, r0, r1)):
        wide_ref[pl.ds(start * 8 + j, block.shape[0], stride=8), :] = piece


def forward_kernel(traces_ref, table_ref, wide_ref, first_ref, last_ref):
    rows = traces_ref.shape[0]
    step = 256

    def one(b, _):
        at = pl.multiple_of(b * step, step)
        spectra = jnp.dot(
            traces_ref[pl.ds(at, step), :], table_ref[...], preferred_element_type=F32
        ).astype(BF16)
        put_sources(wide_ref, at, spectra.astype(F32))

        @pl.when(b == 0)
        def _():
            first_ref[...] = spectra[:HALO]

        @pl.when(b == rows // step - 1)
        def _():
            last_ref[...] = spectra[step - HALO :]

        return 0

    lax.fori_loop(0, rows // step, one, 0)


def fetch_kernel(asked_ref, wide_ref, out_ref, held_ref):
    peers = asked_ref.shape[0]
    sub = lax.broadcasted_iota(jnp.int32, (8, 128), 0)

    def one(p, _):
        base = pl.multiple_of(p * (DISTINCT * 4), DISTINCT * 4)
        for k in range(0, DISTINCT, 2):
            a = wide_ref[asked_ref[p, 0, k]]
            b = pltpu.roll(wide_ref[asked_ref[p, 0, k + 1]], 4, 0)
            held_ref[pl.ds(base + 4 * k, 8), :] = jnp.where(sub < 4, a, b)
        out_ref[pl.ds(base, DISTINCT * 4), :] = held_ref[pl.ds(base, DISTINCT * 4), :].astype(BF16)
        return 0

    lax.fori_loop(0, peers, one, 0)


def slots_kernel(place_ref, rcv_ref, out_ref):
    outs, aper = rcv_ref.shape

    def one(o, _):
        for a in range(aper):
            slot = rcv_ref[o, a]
            out_ref[o, a] = place_ref[slot]
        return 0

    lax.fori_loop(0, outs, one, 0)


def pairs_kernel(
    src_ref, rcv_ref, weight_ref, wide_ref, before_ref, after_ref, arrived_ref, synth_ref, out_ref,
    source_ref, receiver_ref, sum_ref, sem,
):
    outs, aper = src_ref.shape
    own = wide_ref.shape[0] // 8
    copy = pltpu.make_async_copy(wide_ref, source_ref.at[pl.ds(HALO * 8, own * 8)], sem)
    copy.start()
    put_sources(source_ref, 0, before_ref[...].astype(F32))
    put_sources(source_ref, own + HALO, after_ref[...].astype(F32))
    step = 64
    sub = lax.broadcasted_iota(jnp.int32, (8, 128), 0)

    def widen(b, _):
        at = pl.multiple_of(b * (step * 4), step * 4)
        rows = arrived_ref[pl.ds(at, step * 4), :].astype(F32)
        for k in range(0, step, 2):
            x = rows[4 * k : 4 * k + 8]
            y = pltpu.roll(x, 4, 0)
            to = pl.multiple_of(at * 2, step * 8) + 8 * k
            receiver_ref[pl.ds(to, 8), :] = jnp.where(sub < 4, x, y)
            receiver_ref[pl.ds(to + 8, 8), :] = jnp.where(sub < 4, y, x)
        return 0

    lax.fori_loop(0, arrived_ref.shape[0] // (step * 4), widen, 0)
    copy.wait()

    def one(o, _):
        totals = [jnp.zeros((8, 128), F32) for _ in range(4)]

        def some(c, totals):
            totals = list(totals)
            for u in range(16):
                a = c * 16 + u
                s = source_ref[pl.ds(pl.multiple_of(src_ref[o, a], 8), 8), :]
                r = receiver_ref[pl.ds(pl.multiple_of(rcv_ref[o, a], 8), 8), :]
                totals[u % 4] += (s * r) * weight_ref[o, a]
            return tuple(totals)

        totals = lax.fori_loop(0, aper // 16, some, tuple(totals))
        total = (totals[0] + totals[1]) + (totals[2] + totals[3])
        sum_ref[o] = total
        return 0

    lax.fori_loop(0, outs, one, 0)
    pieces = [sum_ref[:, j, :] for j in range(8)]
    summed = jnp.concatenate(
        [pieces[0] - pieces[2], pieces[1] - pieces[3], pieces[4] + pieces[6], pieces[5] + pieces[7]],
        axis=1,
    ).astype(BF16)
    out_ref[...] = jnp.dot(summed, synth_ref[...], preferred_element_type=F32).astype(BF16)


VMEM = pl.BlockSpec(memory_space=pltpu.VMEM)
SMEM = pl.BlockSpec(memory_space=pltpu.SMEM)
ANY = pl.BlockSpec(memory_space=pl.ANY)


def shape(dims, kind):
    return jax.ShapeDtypeStruct(dims, kind)


def params(mib):
    return pltpu.CompilerParams(vmem_limit_bytes=mib << 20)


def body(traces, src_index, rcv_index, taper_index, fetch_rows, line_owner, taper_table):
    sails = lax.axis_size("sail")
    cables = lax.axis_size("cable")
    tr_rows, samples = traces.shape
    outs, aper = src_index.shape
    cap = fetch_rows.shape[1]
    asked, place = pl.pallas_call(
        distinct_kernel,
        in_specs=[SMEM, VMEM],
        out_specs=[VMEM, VMEM],
        out_shape=[shape((sails, 1, cap), jnp.int32), shape((sails, cap), jnp.int32)],
        compiler_params=params(8),
        name="distinct",
    )(line_owner, fetch_rows)
    asked = lax.all_to_all(asked, "sail", split_axis=0, concat_axis=0, tiled=True)
    wide, first, last = pl.pallas_call(
        forward_kernel,
        in_specs=[VMEM, VMEM],
        out_specs=[VMEM, VMEM, VMEM],
        out_shape=[
            shape((tr_rows * 8, 128), F32),
            shape((HALO, samples), BF16),
            shape((HALO, samples), BF16),
        ],
        compiler_params=params(24),
        name="forward",
        cost_estimate=pl.CostEstimate(
            flops=2 * tr_rows * samples * samples, bytes_accessed=12 << 20, transcendentals=0
        ),
    )(traces, forward_table(samples))
    outgoing = pl.pallas_call(
        fetch_kernel,
        in_specs=[SMEM, VMEM],
        out_specs=VMEM,
        out_shape=shape((sails * DISTINCT * 4, 128), BF16),
        scratch_shapes=[pltpu.VMEM((sails * DISTINCT * 4, 128), F32)],
        compiler_params=params(32),
        name="fetch",
    )(asked, wide.reshape(tr_rows, 8, 128))
    arrived = lax.all_to_all(
        outgoing.reshape(sails, DISTINCT * 4, 128), "sail", split_axis=0, concat_axis=0, tiled=True
    ).reshape(sails * DISTINCT * 4, 128)
    up = [(i, i + 1) for i in range(cables - 1)]
    before = lax.ppermute(last, "cable", up)
    after = lax.ppermute(first, "cable", [(j, i) for i, j in up])
    rcv_rows = pl.pallas_call(
        slots_kernel,
        in_specs=[SMEM, SMEM],
        out_specs=SMEM,
        out_shape=shape((outs, aper), jnp.int32),
        name="slots",
        cost_estimate=pl.CostEstimate(flops=0, bytes_accessed=32 << 20, transcendentals=0),
    )(place.reshape(-1) * 8, rcv_index)
    taper_ids = jnp.arange(taper_table.shape[0], dtype=jnp.int32)
    weights = jnp.sum(
        jnp.where(taper_index[..., None] == taper_ids, taper_table, jnp.zeros_like(taper_table)),
        axis=-1,
    )
    return pl.pallas_call(
        pairs_kernel,
        in_specs=[SMEM, SMEM, SMEM, ANY, VMEM, VMEM, VMEM, VMEM],
        out_specs=VMEM,
        out_shape=shape((outs, samples), BF16),
        scratch_shapes=[
            pltpu.VMEM(((tr_rows + 2 * HALO) * 8, 128), F32),
            pltpu.VMEM((sails * DISTINCT * 8, 128), F32),
            pltpu.VMEM((outs, 8, 128), F32),
            pltpu.SemaphoreType.DMA,
        ],
        compiler_params=params(32),
        name="pairs",
    )(src_index * 8, rcv_rows, weights, wide, before, after, arrived, synthesis_table(samples, aper))


def solution(mesh):
    split = P(("sail", "cable"), None)
    return jax.shard_map(
        body,
        mesh=mesh,
        in_specs=(split, split, split, split, split, P(), P()),
        out_specs=split,
        check_vma=False,
    )
```

```python
import math

import jax
import jax.numpy as jnp
import ml_dtypes
import numpy as np
from jax import lax
from jax.experimental import pallas as pl
from jax.experimental.pallas import tpu as pltpu
from jax.sharding import PartitionSpec as P

HALO = 64
DISTINCT = 64
PAD = 8
TILE = 256
CHUNKS = 4
F32 = jnp.float32
BF16 = jnp.bfloat16


def forward_table(samples):
    turns = np.arange(samples)[:, None] * np.arange(samples // 2)[None, :] % samples
    angle = turns * (2.0 * math.pi / samples)
    table = np.concatenate([np.cos(angle), -np.sin(angle)], axis=1) / math.sqrt(samples)
    return jnp.asarray(table.astype(np.float32).astype(ml_dtypes.bfloat16))


def synthesis_table(samples, aperture):
    turns = np.arange(samples // 2)[:, None] * np.arange(samples)[None, :] % samples
    angle = turns * (2.0 * math.pi / samples)
    scale = math.sqrt(aperture * (samples // 2))
    table = np.concatenate([np.cos(angle), -np.sin(angle)], axis=0) / scale
    return jnp.asarray(table.astype(np.float32).astype(ml_dtypes.bfloat16))


def distinct_kernel(owner_ref, rows_ref, asked_ref, place_ref):
    lines, cap = rows_ref.shape
    rows = rows_ref[...]
    sub = lax.broadcasted_iota(jnp.int32, (cap, cap), 0)
    lane = lax.broadcasted_iota(jnp.int32, (cap, cap), 1)
    pad = jnp.zeros((cap - lines, cap), jnp.int32)

    def turned(values):
        return jnp.concatenate([values, pad], axis=0).T

    columns = turned(rows)
    once = []
    for g in range(lines):
        column = columns[:, g : g + 1]
        row = rows[g : g + 1, :]
        repeats = jnp.sum(((column == row) & (sub < lane)).astype(jnp.int32), axis=0, keepdims=True)
        once.append(jnp.where(repeats == 0, row, 1 << 20))
    once_columns = turned(jnp.concatenate(once, axis=0))
    ranks = []
    for g in range(lines):
        smaller = (once_columns[:, g : g + 1] < rows[g : g + 1, :]).astype(jnp.int32)
        ranks.append(jnp.sum(smaller, axis=0, keepdims=True))
    rank_columns = turned(jnp.concatenate(ranks, axis=0))
    for g in range(lines):
        match = rank_columns[:, g : g + 1] == lane
        picked = jnp.max(jnp.where(match, columns[:, g : g + 1], 0), axis=0, keepdims=True)
        asked_ref[owner_ref[g]] = picked * 4
        place_ref[g : g + 1, :] = ranks[g] + owner_ref[g] * DISTINCT


def put_rows(ref, start, block):
    for q in range(4):
        at = pl.ds(start + q, block.shape[0], stride=4)
        ref[at, :] = block[:, 128 * q : 128 * (q + 1)]


def forward_kernel(traces_ref, table_ref, rows_ref, first_ref, last_ref):
    step = pl.program_id(0)
    spectra = jnp.dot(traces_ref[...], table_ref[...], preferred_element_type=F32).astype(BF16)
    put_rows(rows_ref, 0, spectra.astype(F32))

    @pl.when(step == 0)
    def _():
        first_ref[...] = spectra[:HALO]

    @pl.when(step == pl.num_programs(0) - 1)
    def _():
        last_ref[...] = spectra[spectra.shape[0] - HALO :]


def gather_rows(index, rows_ref, held_ref, out_ref, base, count):
    sub = lax.broadcasted_iota(jnp.int32, (8, 128), 0)
    for k in range(0, count, 2):
        a = rows_ref[pl.ds(index(k) + PAD, 8), :]
        b = rows_ref[pl.ds(index(k + 1) + PAD - 4, 8), :]
        held_ref[pl.ds(pl.multiple_of(base * 4, 8) + 4 * k, 8), :] = jnp.where(sub < 4, a, b)
    for q in range(4):
        part = held_ref[pl.ds(base * 4 + q, count, stride=4), :]
        out_ref[pl.ds(base, count), 128 * q : 128 * (q + 1)] = part.astype(BF16)


def fetch_kernel(asked_ref, rows_ref, out_ref, own_ref, held_ref, sem):
    own = rows_ref.shape[0]
    copy = pltpu.make_async_copy(rows_ref, own_ref.at[pl.ds(PAD, own)], sem)
    copy.start()
    copy.wait()

    def one(p, _):
        base = pl.multiple_of(p * DISTINCT, DISTINCT)
        gather_rows(lambda k: asked_ref[p, 0, k], own_ref, held_ref, out_ref, base, DISTINCT)
        return 0

    lax.fori_loop(0, asked_ref.shape[0], one, 0)


def slots_kernel(place_ref, src_ref, rcv_ref, taper_ref, key_ref, value_ref):
    lines, cap = place_ref.shape
    outs = rcv_ref.shape[0]
    place = place_ref[...]
    rank = (place & (DISTINCT - 1)).astype(F32).astype(BF16)
    first = (place - (place & (DISTINCT - 1))).astype(F32)
    sub = lax.broadcasted_iota(jnp.int32, (cap, cap), 0)
    line = lax.broadcasted_iota(jnp.int32, (lines, cap), 0)

    def some(b, _):
        at = pl.multiple_of(b * 8, 8)
        slots = rcv_ref[pl.ds(at, 8), :]
        rows = []
        for u in range(8):
            slot = slots[u : u + 1, :]
            at_slot = (sub == (slot & (cap - 1))).astype(F32).astype(BF16)
            found = jnp.dot(rank, at_slot, preferred_element_type=F32) + first
            rows.append(
                jnp.sum(jnp.where(line == slot // cap, found, 0.0), axis=0, keepdims=True)
            )
        rows = jnp.concatenate(rows, axis=0).astype(jnp.int32)
        out = lax.broadcasted_iota(jnp.int32, (8, cap), 0) + at
        key_ref[pl.ds(at, 8), :] = (rows * outs + out) * 16 + taper_ref[pl.ds(at, 8), :]
        value_ref[pl.ds(at, 8), :] = src_ref[pl.ds(at, 8), :] * 4
        return 0

    lax.fori_loop(0, outs // 8, some, 0)


def sources_kernel(
    src_ref, ends_ref, rows_ref, before_ref, after_ref, out_ref, tile_ref, block_ref, all_ref, held_ref, sem
):
    step = pl.program_id(0)

    @pl.when(step == 0)
    def _():
        own = rows_ref.shape[0]
        copy = pltpu.make_async_copy(rows_ref, all_ref.at[pl.ds(PAD + HALO * 4, own)], sem)
        copy.start()
        put_rows(all_ref, PAD, before_ref[...].astype(F32))
        put_rows(all_ref, PAD + HALO * 4 + own, after_ref[...].astype(F32))
        tiles = ends_ref.shape[1]
        meets = tile_ref.shape[0]

        def blank(e, _):
            tile_ref[e] = tiles - 1
            block_ref[e] = meets - tiles
            return 0

        lax.fori_loop(0, meets, blank, 0)

        def meet(t, count):
            def add(b, count):
                tile_ref[count] = t
                block_ref[count] = b
                return count + 1

            return lax.fori_loop(ends_ref[0, t], ends_ref[1, t] + 1, add, count)

        lax.fori_loop(0, tiles, meet, 0)
        copy.wait()

    def one(c, _):
        base = pl.multiple_of(c * 64, 64)
        first = step * out_ref.shape[0] + base
        gather_rows(lambda k: src_ref[first + k], all_ref, held_ref, out_ref, base, 64)
        return 0

    lax.fori_loop(0, out_ref.shape[0] // 64, one, 0)


def plan_kernel(taper_ref, key_ref, local_ref, weight_ref, block_ref):
    outs, cap = key_ref.shape
    key = key_ref[...]
    rows = key // (16 * outs)
    local = (rows & (TILE - 1)).T
    lane = lax.broadcasted_iota(jnp.int32, (cap, TILE), 1)
    entry = key & 15
    weights = jnp.zeros(key.shape, F32)
    for k in range(taper_ref.shape[0]):
        weights = jnp.where(entry == k, taper_ref[k], weights)
    out = (key // 16) & (outs - 1)
    blocks = rows // TILE
    sub = lax.broadcasted_iota(jnp.int32, (outs, cap), 0)
    per = TILE // cap
    for o in range(outs):
        hot = (local[:, o : o + 1] == lane).astype(F32).astype(BF16)
        local_ref[o // per, cap * (o % per) : cap * (o % per + 1), :] = hot
        at = slice(cap * (o % per), cap * (o % per + 1))
        spread = jnp.where(sub == out[o : o + 1, :], weights[o : o + 1, :], 0.0)
        weight_ref[o // per, :, at] = spread.astype(BF16)
        block_ref[o // per, :, at] = jnp.broadcast_to(blocks[o : o + 1, :], (8, cap))


def pairs_kernel(
    tile_ref, meet_ref, local_hbm, weight_hbm, block_hbm, source_hbm, arrived_ref, synth_ref, out_ref,
    local_ref, weight_ref, block_ref, source_ref, sum_ref, sems,
):
    half = source_ref.shape[2] // 2
    last = arrived_ref.shape[0] // TILE - 1
    chunk = local_ref.shape[0] // CHUNKS
    unroll = 4
    held = ((local_hbm, local_ref), (weight_hbm, weight_ref), (block_hbm, block_ref), (source_hbm, source_ref))

    def copies(c):
        at = pl.ds(c * chunk, chunk)
        return [
            pltpu.make_async_copy(a.at[at], b.at[at], sems.at[i, c]) for i, (a, b) in enumerate(held)
        ]

    for c in range(CHUNKS):
        for copy in copies(c):
            copy.start()
    sum_ref[...] = jnp.zeros_like(sum_ref)

    def some(c, _):
        @pl.when((c * unroll % chunk == 0) & (c * unroll < chunk * CHUNKS))
        def _():
            for copy in copies(c * unroll // chunk):
                copy.wait()

        total = sum_ref[...]
        for u in range(unroll):
            t = tile_ref[c * unroll + u]
            b = meet_ref[c * unroll + u]
            at = pl.multiple_of(jnp.minimum(b, last) * TILE, TILE)
            right = jnp.dot(
                local_ref[t], arrived_ref[pl.ds(at, TILE), :], preferred_element_type=F32
            )
            left = source_ref[t].astype(F32)
            sr, si, rr, ri = left[:, :half], left[:, half:], right[:, :half], right[:, half:]
            product = jnp.concatenate([sr * rr - si * ri, sr * ri + si * rr], axis=1).astype(BF16)
            weight = weight_ref[t]
            here = block_ref[t][:1, :] == b
            weight = jnp.where(here, weight.astype(F32), 0.0).astype(BF16)
            total += jnp.dot(weight, product, preferred_element_type=F32)
        sum_ref[...] = total
        return 0

    lax.fori_loop(0, tile_ref.shape[0] // unroll, some, 0)
    summed = sum_ref[...].astype(BF16)
    out_ref[...] = jnp.dot(summed, synth_ref[...], preferred_element_type=F32).astype(BF16)


VMEM = pl.BlockSpec(memory_space=pltpu.VMEM)
SMEM = pl.BlockSpec(memory_space=pltpu.SMEM)
HBM = pl.BlockSpec(memory_space=pltpu.HBM)


def shape(dims, kind):
    return jax.ShapeDtypeStruct(dims, kind)


def params(mib):
    return pltpu.CompilerParams(vmem_limit_bytes=mib << 20)


def cost(flops, moved):
    return pl.CostEstimate(flops=flops, bytes_accessed=moved, transcendentals=0)


def body(traces, src_index, rcv_index, taper_index, fetch_rows, line_owner, taper_table):
    sails = lax.axis_size("sail")
    cables = lax.axis_size("cable")
    tr_rows, samples = traces.shape
    outs, aper = src_index.shape
    cap = fetch_rows.shape[1]
    asked, place = pl.pallas_call(
        distinct_kernel,
        in_specs=[SMEM, VMEM],
        out_specs=[VMEM, VMEM],
        out_shape=[shape((sails, 1, cap), jnp.int32), shape((sails, cap), jnp.int32)],
        compiler_params=params(56),
        name="distinct",
    )(line_owner, fetch_rows)
    asked = lax.all_to_all(asked, "sail", split_axis=0, concat_axis=0, tiled=True)
    step = 256
    rows, first, last = pl.pallas_call(
        forward_kernel,
        grid=(tr_rows // step,),
        in_specs=[
            pl.BlockSpec((step, samples), lambda b: (b, 0)),
            pl.BlockSpec((samples, samples), lambda b: (0, 0)),
        ],
        out_specs=[
            pl.BlockSpec((step * 4, 128), lambda b: (b, 0)),
            pl.BlockSpec((HALO, samples), lambda b: (0, 0)),
            pl.BlockSpec((HALO, samples), lambda b: (0, 0)),
        ],
        out_shape=[
            shape((tr_rows * 4, 128), F32),
            shape((HALO, samples), BF16),
            shape((HALO, samples), BF16),
        ],
        compiler_params=params(56),
        name="forward",
        cost_estimate=cost(2 * tr_rows * samples * samples, 8 << 20),
    )(traces, forward_table(samples))
    fetched = sails * DISTINCT
    outgoing = pl.pallas_call(
        fetch_kernel,
        in_specs=[SMEM, HBM],
        out_specs=VMEM,
        out_shape=shape((fetched, samples), BF16),
        scratch_shapes=[
            pltpu.VMEM((tr_rows * 4 + 2 * PAD, 128), F32),
            pltpu.VMEM((fetched * 4, 128), F32),
            pltpu.SemaphoreType.DMA,
        ],
        compiler_params=params(50),
        name="fetch",
    )(asked, rows)
    arrived = lax.all_to_all(
        outgoing.reshape(sails, DISTINCT, samples), "sail", split_axis=0, concat_axis=0, tiled=True
    ).reshape(fetched, samples)
    up = [(i, i + 1) for i in range(cables - 1)]
    before = lax.ppermute(last, "cable", up)
    after = lax.ppermute(first, "cable", [(j, i) for i, j in up])
    key, value = pl.pallas_call(
        slots_kernel,
        in_specs=[VMEM] * 4,
        out_specs=[VMEM, VMEM],
        out_shape=[shape((outs, aper), jnp.int32)] * 2,
        compiler_params=params(56),
        name="slots",
        cost_estimate=cost(0, 10 << 20),
    )(place, src_index, rcv_index, taper_index)
    count = outs * aper
    key, value = lax.sort((key.reshape(-1), value.reshape(-1)), num_keys=1, is_stable=False)
    tiles = count // TILE
    blocks = fetched // TILE
    ends = key.reshape(tiles, TILE)[:, :: TILE - 1].T // (16 * outs * TILE)
    meets = tiles + blocks
    sources, tile, meet = pl.pallas_call(
        sources_kernel,
        grid=(8,),
        in_specs=[SMEM, SMEM, HBM, VMEM, VMEM],
        out_specs=[pl.BlockSpec((count // 8, samples), lambda b: (b, 0)), SMEM, SMEM],
        out_shape=[
            shape((count, samples), BF16), shape((meets,), jnp.int32), shape((meets,), jnp.int32)
        ],
        scratch_shapes=[
            pltpu.VMEM(((tr_rows + 2 * HALO) * 4 + 2 * PAD, 128), F32),
            pltpu.VMEM((count // 8 * 4, 128), F32),
            pltpu.SemaphoreType.DMA,
        ],
        compiler_params=params(56),
        name="sources",
        cost_estimate=cost(0, 40 << 20),
    )(value, ends, rows, before, after)
    local, weights, where = pl.pallas_call(
        plan_kernel,
        in_specs=[SMEM, VMEM],
        out_specs=[VMEM, VMEM, VMEM],
        out_shape=[
            shape((tiles, TILE, TILE), BF16),
            shape((tiles, outs, TILE), BF16),
            shape((tiles, 8, TILE), jnp.int32),
        ],
        compiler_params=params(56),
        name="plan",
        cost_estimate=cost(0, 10 << 20),
    )(taper_table, key.reshape(outs, aper))
    return pl.pallas_call(
        pairs_kernel,
        in_specs=[SMEM, SMEM, HBM, HBM, HBM, HBM, VMEM, VMEM],
        out_specs=VMEM,
        out_shape=shape((outs, samples), BF16),
        scratch_shapes=[
            pltpu.VMEM((tiles, TILE, TILE), BF16),
            pltpu.VMEM((tiles, outs, TILE), BF16),
            pltpu.VMEM((tiles, 8, TILE), jnp.int32),
            pltpu.VMEM((tiles, TILE, samples), BF16),
            pltpu.VMEM((outs, samples), F32),
            pltpu.SemaphoreType.DMA((4, CHUNKS)),
        ],
        compiler_params=params(50),
        name="pairs",
    )(
        tile, meet, local, weights, where, sources.reshape(tiles, TILE, samples), arrived,
        synthesis_table(samples, aper),
    )


def solution(mesh):
    split = P(("sail", "cable"), None)
    return jax.shard_map(
        body,
        mesh=mesh,
        in_specs=(split, split, split, split, split, P(), P()),
        out_specs=split,
        check_vma=False,
    )
```

```python
import math

import jax
import jax.numpy as jnp
import ml_dtypes
import numpy as np
from jax import lax
from jax.experimental import pallas as pl
from jax.experimental.pallas import tpu as pltpu
from jax.sharding import PartitionSpec as P

HALO = 64
DISTINCT = 64
PAD = 8
TILE = 256
STEP = 512
GROUPS = 4
CHUNKS = 8
UNROLL = 8
F32 = jnp.float32
BF16 = jnp.bfloat16


def forward_table(samples):
    turns = np.arange(samples)[:, None] * np.arange(samples // 2)[None, :] % samples
    angle = turns * (2.0 * math.pi / samples)
    table = np.concatenate([np.cos(angle), -np.sin(angle)], axis=1) / math.sqrt(samples)
    return jnp.asarray(table.astype(np.float32).astype(ml_dtypes.bfloat16))


def synthesis_table(samples, aperture):
    turns = np.arange(samples // 2)[:, None] * np.arange(samples)[None, :] % samples
    angle = turns * (2.0 * math.pi / samples)
    scale = math.sqrt(aperture * (samples // 2))
    table = np.concatenate([np.cos(angle), -np.sin(angle)], axis=0) / scale
    return jnp.asarray(table.astype(np.float32).astype(ml_dtypes.bfloat16))


def turned(values):
    lines, cap = values.shape
    return jnp.concatenate([values, jnp.zeros((cap - lines, cap), values.dtype)], axis=0).T


def distinct_kernel(owner_ref, rows_ref, asked_ref, place_ref):
    lines, cap = rows_ref.shape
    rows = rows_ref[...]
    sub = lax.broadcasted_iota(jnp.int32, (cap, cap), 0)
    lane = lax.broadcasted_iota(jnp.int32, (cap, cap), 1)
    earlier = sub < lane
    columns = turned(rows)
    repeats = []
    for g in range(lines):
        same = (columns[:, g : g + 1] == rows[g : g + 1, :]) & earlier
        repeats.append(jnp.max(jnp.where(same, 1.0, 0.0), axis=0, keepdims=True))
    once = 1.0 - jnp.concatenate(repeats, axis=0)
    before = jnp.where(earlier, 1.0, 0.0).astype(BF16)
    place = jnp.dot(once.astype(BF16), before, preferred_element_type=F32)
    place = jnp.where(once > 0.0, place, -1.0).astype(jnp.int32)
    place_ref[...] = place
    places = turned(place)
    for g in range(lines):
        match = places[:, g : g + 1] == lane
        picked = jnp.max(jnp.where(match, columns[:, g : g + 1], 0), axis=0, keepdims=True)
        asked_ref[owner_ref[g]] = picked * 4


def put_rows(ref, start, block):
    for q in range(4):
        at = pl.ds(start + q, block.shape[0], stride=4)
        ref[at, :] = block[:, 128 * q : 128 * (q + 1)]


def gather_rows(index, rows_ref, held_ref, out_ref, base, count):
    sub = lax.broadcasted_iota(jnp.int32, (8, 128), 0)
    for k in range(0, count, 2):
        a = rows_ref[pl.ds(index(k) + PAD, 8), :]
        b = rows_ref[pl.ds(index(k + 1) + PAD - 4, 8), :]
        held_ref[pl.ds(pl.multiple_of(base * 4, 8) + 4 * k, 8), :] = jnp.where(sub < 4, a, b)
    for q in range(4):
        part = held_ref[pl.ds(base * 4 + q, count, stride=4), :]
        out_ref[pl.ds(base, count), 128 * q : 128 * (q + 1)] = part.astype(BF16)


def spectra_kernel(
    asked_ref, traces_hbm, table_ref, rows_hbm, first_ref, last_ref, out_hbm,
    traces_ref, rows_ref, held_ref, out_ref, in_sems, row_sems, out_sems,
):
    parts = len(range(0, traces_ref.shape[0], STEP))
    loads = []
    stores = []
    for b in range(parts):
        at = pl.ds(b * STEP, STEP)
        loads.append(pltpu.make_async_copy(traces_hbm.at[at], traces_ref.at[at], in_sems.at[b]))
        stores.append(
            pltpu.make_async_copy(
                rows_ref.at[pl.ds(PAD + b * STEP * 4, STEP * 4)],
                rows_hbm.at[pl.ds(b * STEP * 4, STEP * 4)],
                row_sems.at[b],
            )
        )
        loads[b].start()
    for b in range(parts):
        loads[b].wait()
        spectra = jnp.dot(
            traces_ref[b * STEP : (b + 1) * STEP, :], table_ref[...], preferred_element_type=F32
        ).astype(BF16)
        put_rows(rows_ref, PAD + b * STEP * 4, spectra.astype(F32))
        if b == 0:
            first_ref[...] = spectra[:HALO]
        if b == parts - 1:
            last_ref[...] = spectra[STEP - HALO :]
    peers = asked_ref.shape[0]
    each = peers // GROUPS
    sends = []
    for g in range(GROUPS):

        def one(p, _):
            base = pl.multiple_of(p * DISTINCT, DISTINCT)
            gather_rows(lambda k: asked_ref[p, 0, k], rows_ref, held_ref, out_ref, base, DISTINCT)
            return 0

        lax.fori_loop(g * each, (g + 1) * each, one, 0)
        at = pl.ds(g * each * DISTINCT, each * DISTINCT)
        sends.append(pltpu.make_async_copy(out_ref.at[at], out_hbm.at[at], out_sems.at[g]))
        sends[g].start()
    for b in range(parts):
        stores[b].start()
    for copy in sends + stores:
        copy.wait()


def slots_kernel(
    owner_ref, rows_ref, place_ref, src_ref, rcv_ref, taper_ref, key_ref, value_ref, rank_ref
):
    lines, cap = place_ref.shape
    outs = rcv_ref.shape[0]
    rows = rows_ref[...]
    columns = turned(rows)
    places = turned(place_ref[...])
    for g in range(lines):
        same = columns[:, g : g + 1] == rows[g : g + 1, :]
        rank_ref[g : g + 1, :] = jnp.max(
            jnp.where(same, places[:, g : g + 1], -1), axis=0, keepdims=True
        )
    line = lax.broadcasted_iota(jnp.int32, (lines, cap), 0)
    first = jnp.zeros((lines, cap), F32)
    for g in range(lines):
        first = jnp.where(line == g, (owner_ref[g] * DISTINCT).astype(F32), first)
    rank = rank_ref[...].astype(F32).astype(BF16)
    sub = lax.broadcasted_iota(jnp.int32, (cap, cap), 0)

    def some(b, _):
        at = pl.multiple_of(b * 8, 8)
        slots = rcv_ref[pl.ds(at, 8), :]
        rows = []
        for u in range(8):
            slot = slots[u : u + 1, :]
            at_slot = (sub == (slot & (cap - 1))).astype(F32).astype(BF16)
            found = jnp.dot(rank, at_slot, preferred_element_type=F32) + first
            rows.append(
                jnp.sum(jnp.where(line == slot // cap, found, 0.0), axis=0, keepdims=True)
            )
        rows = jnp.concatenate(rows, axis=0).astype(jnp.int32)
        out = lax.broadcasted_iota(jnp.int32, (8, cap), 0) + at
        key_ref[pl.ds(at, 8), :] = (rows * outs + out) * 16 + taper_ref[pl.ds(at, 8), :]
        value_ref[pl.ds(at, 8), :] = src_ref[pl.ds(at, 8), :] * 4
        return 0

    lax.fori_loop(0, outs // 8, some, 0)


def sources_kernel(
    src_ref, ends_ref, rows_ref, before_ref, after_ref, out_ref, meet_ref, all_ref, held_ref, sem
):
    step = pl.program_id(0)

    @pl.when(step == 0)
    def _():
        own = rows_ref.shape[0]
        copy = pltpu.make_async_copy(rows_ref, all_ref.at[pl.ds(PAD + HALO * 4, own)], sem)
        copy.start()
        put_rows(all_ref, PAD, before_ref[...].astype(F32))
        put_rows(all_ref, PAD + HALO * 4 + own, after_ref[...].astype(F32))
        tiles = ends_ref.shape[1]
        meets = meet_ref.shape[0]

        def blank(e, _):
            meet_ref[e] = (meets - tiles) * 64 + tiles - 1
            return 0

        lax.fori_loop(0, meets, blank, 0)

        def meet(t, count):
            def add(b, count):
                meet_ref[count] = b * 64 + t
                return count + 1

            return lax.fori_loop(ends_ref[0, t], ends_ref[1, t] + 1, add, count)

        lax.fori_loop(0, tiles, meet, 0)
        copy.wait()

    def one(c, _):
        base = pl.multiple_of(c * 64, 64)
        first = step * out_ref.shape[0] + base
        gather_rows(lambda k: src_ref[first + k], all_ref, held_ref, out_ref, base, 64)
        return 0

    lax.fori_loop(0, out_ref.shape[0] // 64, one, 0)


def pairs_kernel(
    meet_ref, key_ref, taper_ref, source_hbm, arrived_ref, synth_hbm, out_ref,
    source_ref, synth_ref, sum_ref, weight_ref, hot_ref, product_ref, sems, synth_sem,
):
    tiles, _, samples = source_ref.shape
    outs = out_ref.shape[0]
    half = samples // 2
    last = arrived_ref.shape[0] // TILE - 1
    chunk = tiles // CHUNKS

    def load(c):
        at = pl.ds(c * chunk, chunk)
        return pltpu.make_async_copy(source_hbm.at[at], source_ref.at[at], sems.at[c])

    for c in range(CHUNKS):
        load(c).start()
    synth_copy = pltpu.make_async_copy(synth_hbm, synth_ref, synth_sem)
    synth_copy.start()
    entry = key_ref[...] & 15
    weights = jnp.zeros(entry.shape, F32)
    for k in range(taper_ref.shape[0]):
        weights = jnp.where(entry == k, taper_ref[k], weights)
    weight_ref[...] = weights
    sum_ref[...] = jnp.zeros_like(sum_ref)
    sub = lax.broadcasted_iota(jnp.int32, (TILE, TILE), 0)
    out = lax.broadcasted_iota(jnp.int32, (outs, TILE), 0)

    def some(c, _):
        @pl.when(c * UNROLL < tiles)
        def _():
            for u in range(UNROLL // chunk):
                load(c * (UNROLL // chunk) + u).wait()

        for u in range(UNROLL):
            meet = meet_ref[c * UNROLL + u]
            t = meet & 63
            b = meet // 64
            at = pl.multiple_of(jnp.minimum(b, last) * TILE, TILE)
            key = key_ref[pl.ds(t, 1), :]
            row = key // (16 * outs)
            here = jnp.where(row // TILE == b, weight_ref[pl.ds(t, 1), :], 0.0)
            spread = jnp.where(out == ((key // 16) & (outs - 1)), here, 0.0).astype(BF16)
            hot = jnp.where(sub == (row & (TILE - 1)), 1.0, 0.0).astype(BF16)
            right = lax.dot_general(
                hot, arrived_ref[pl.ds(at, TILE), :], (((0,), (0,)), ((), ())),
                preferred_element_type=F32,
            )
            left = source_ref[t].astype(F32)
            sr, si, rr, ri = left[:, :half], left[:, half:], right[:, :half], right[:, half:]
            product = jnp.concatenate([sr * rr - si * ri, sr * ri + si * rr], axis=1)
            product_ref[u * TILE : (u + 1) * TILE, :] = product.astype(BF16)
            hot_ref[:, u * TILE : (u + 1) * TILE] = spread
        sum_ref[...] += jnp.dot(hot_ref[...], product_ref[...], preferred_element_type=F32)
        return 0

    lax.fori_loop(0, meet_ref.shape[0] // UNROLL, some, 0)
    synth_copy.wait()
    summed = sum_ref[...].astype(BF16)
    out_ref[...] = jnp.dot(summed, synth_ref[...], preferred_element_type=F32).astype(BF16)


VMEM = pl.BlockSpec(memory_space=pltpu.VMEM)
SMEM = pl.BlockSpec(memory_space=pltpu.SMEM)
HBM = pl.BlockSpec(memory_space=pltpu.HBM)


def shape(dims, kind):
    return jax.ShapeDtypeStruct(dims, kind)


def params(mib):
    return pltpu.CompilerParams(vmem_limit_bytes=mib << 20)


def cost(flops, moved):
    return pl.CostEstimate(flops=flops, bytes_accessed=moved, transcendentals=0)


def body(traces, src_index, rcv_index, taper_index, fetch_rows, line_owner, taper_table):
    sails = lax.axis_size("sail")
    cables = lax.axis_size("cable")
    tr_rows, samples = traces.shape
    outs, aper = src_index.shape
    cap = fetch_rows.shape[1]
    asked, place = pl.pallas_call(
        distinct_kernel,
        in_specs=[SMEM, VMEM],
        out_specs=[VMEM, VMEM],
        out_shape=[shape((sails, 1, cap), jnp.int32), shape((sails, cap), jnp.int32)],
        compiler_params=params(56),
        name="distinct",
    )(line_owner, fetch_rows)
    asked = lax.all_to_all(asked, "sail", split_axis=0, concat_axis=0, tiled=True)
    fetched = sails * DISTINCT
    parts = tr_rows // STEP
    rows, first, last, outgoing = pl.pallas_call(
        spectra_kernel,
        in_specs=[SMEM, HBM, VMEM],
        out_specs=[HBM, VMEM, VMEM, HBM],
        out_shape=[
            shape((tr_rows * 4, 128), F32),
            shape((HALO, samples), BF16),
            shape((HALO, samples), BF16),
            shape((fetched, samples), BF16),
        ],
        scratch_shapes=[
            pltpu.VMEM((tr_rows, samples), BF16),
            pltpu.VMEM((tr_rows * 4 + 2 * PAD, 128), F32),
            pltpu.VMEM((fetched * 4, 128), F32),
            pltpu.VMEM((fetched, samples), BF16),
            pltpu.SemaphoreType.DMA((parts,)),
            pltpu.SemaphoreType.DMA((parts,)),
            pltpu.SemaphoreType.DMA((GROUPS,)),
        ],
        compiler_params=params(56),
        name="spectra",
    )(asked, traces, forward_table(samples))
    arrived = lax.all_to_all(
        outgoing.reshape(sails, DISTINCT, samples), "sail", split_axis=0, concat_axis=0, tiled=True
    ).reshape(fetched, samples)
    up = [(i, i + 1) for i in range(cables - 1)]
    before = lax.ppermute(last, "cable", up)
    after = lax.ppermute(first, "cable", [(j, i) for i, j in up])
    key, value = pl.pallas_call(
        slots_kernel,
        in_specs=[SMEM] + [VMEM] * 5,
        out_specs=[VMEM, VMEM],
        out_shape=[shape((outs, aper), jnp.int32)] * 2,
        scratch_shapes=[pltpu.VMEM((sails, cap), jnp.int32)],
        compiler_params=params(56),
        name="slots",
        cost_estimate=cost(0, 10 << 20),
    )(line_owner, fetch_rows, place, src_index, rcv_index, taper_index)
    count = outs * aper
    key, value = lax.sort((key.reshape(-1), value.reshape(-1)), num_keys=1, is_stable=False)
    tiles = count // TILE
    blocks = fetched // TILE
    ends = key.reshape(tiles, TILE)[:, :: TILE - 1].T // (16 * outs * TILE)
    meets = -(-(tiles + blocks) // UNROLL) * UNROLL
    sources, meet = pl.pallas_call(
        sources_kernel,
        grid=(8,),
        in_specs=[SMEM, SMEM, HBM, VMEM, VMEM],
        out_specs=[pl.BlockSpec((count // 8, samples), lambda b: (b, 0)), SMEM],
        out_shape=[shape((count, samples), BF16), shape((meets,), jnp.int32)],
        scratch_shapes=[
            pltpu.VMEM(((tr_rows + 2 * HALO) * 4 + 2 * PAD, 128), F32),
            pltpu.VMEM((count // 8 * 4, 128), F32),
            pltpu.SemaphoreType.DMA,
        ],
        compiler_params=params(56),
        name="sources",
        cost_estimate=cost(0, 40 << 20),
    )(value, ends, rows, before, after)
    return pl.pallas_call(
        pairs_kernel,
        in_specs=[SMEM, VMEM, SMEM, HBM, VMEM, HBM],
        out_specs=VMEM,
        out_shape=shape((outs, samples), BF16),
        scratch_shapes=[
            pltpu.VMEM((tiles, TILE, samples), BF16),
            pltpu.VMEM((samples, samples), BF16),
            pltpu.VMEM((outs, samples), F32),
            pltpu.VMEM((tiles, TILE), F32),
            pltpu.VMEM((outs, UNROLL * TILE), BF16),
            pltpu.VMEM((UNROLL * TILE, samples), BF16),
            pltpu.SemaphoreType.DMA((CHUNKS,)),
            pltpu.SemaphoreType.DMA,
        ],
        compiler_params=params(50),
        name="pairs",
    )(
        meet, key.reshape(tiles, TILE), taper_table, sources.reshape(tiles, TILE, samples), arrived,
        synthesis_table(samples, aper),
    )


def solution(mesh):
    split = P(("sail", "cable"), None)
    return jax.shard_map(
        body,
        mesh=mesh,
        in_specs=(split, split, split, split, split, P(), P()),
        out_specs=split,
        check_vma=False,
    )
```

```python
import math

import jax
import jax.numpy as jnp
import ml_dtypes
import numpy as np
from jax import lax
from jax.experimental import pallas as pl
from jax.experimental.pallas import tpu as pltpu
from jax.sharding import PartitionSpec as P

HALO = 64
DISTINCT = 64
PAD = 8
TILE = 256
STEP = 512
GROUPS = 4
CHUNKS = 8
UNROLL = 8
F32 = jnp.float32
BF16 = jnp.bfloat16


def forward_table(samples):
    turns = np.arange(samples)[:, None] * np.arange(samples // 2)[None, :] % samples
    angle = turns * (2.0 * math.pi / samples)
    table = np.concatenate([np.cos(angle), -np.sin(angle)], axis=1) / math.sqrt(samples)
    return jnp.asarray(table.astype(np.float32).astype(ml_dtypes.bfloat16))


def synthesis_table(samples, aperture):
    turns = np.arange(samples // 2)[:, None] * np.arange(samples)[None, :] % samples
    angle = turns * (2.0 * math.pi / samples)
    scale = math.sqrt(aperture * (samples // 2))
    table = np.concatenate([np.cos(angle), -np.sin(angle)], axis=0) / scale
    return jnp.asarray(table.astype(np.float32).astype(ml_dtypes.bfloat16))


def turned(values):
    lines, cap = values.shape
    return jnp.concatenate([values, jnp.zeros((cap - lines, cap), values.dtype)], axis=0).T


def distinct_kernel(owner_ref, rows_ref, asked_ref, place_ref):
    lines, cap = rows_ref.shape
    rows = rows_ref[...]
    sub = lax.broadcasted_iota(jnp.int32, (cap, cap), 0)
    lane = lax.broadcasted_iota(jnp.int32, (cap, cap), 1)
    earlier = sub < lane
    columns = turned(rows)
    repeats = []
    for g in range(lines):
        same = (columns[:, g : g + 1] == rows[g : g + 1, :]) & earlier
        repeats.append(jnp.max(jnp.where(same, 1.0, 0.0), axis=0, keepdims=True))
    once = 1.0 - jnp.concatenate(repeats, axis=0)
    before = jnp.where(earlier, 1.0, 0.0).astype(BF16)
    place = jnp.dot(once.astype(BF16), before, preferred_element_type=F32)
    place = jnp.where(once > 0.0, place, -1.0).astype(jnp.int32)
    place_ref[...] = place
    places = turned(place)
    for g in range(lines):
        match = places[:, g : g + 1] == lane
        picked = jnp.max(jnp.where(match, columns[:, g : g + 1], 0), axis=0, keepdims=True)
        asked_ref[owner_ref[g]] = picked * 4


def put_rows(ref, start, block):
    for q in range(4):
        at = pl.ds(start + q, block.shape[0], stride=4)
        ref[at, :] = block[:, 128 * q : 128 * (q + 1)]


def gather_rows(index, rows_ref, held_ref, out_ref, base, count):
    sub = lax.broadcasted_iota(jnp.int32, (8, 128), 0)
    for k in range(0, count, 2):
        a = rows_ref[pl.ds(index(k) + PAD, 8), :]
        b = rows_ref[pl.ds(index(k + 1) + PAD - 4, 8), :]
        held_ref[pl.ds(pl.multiple_of(base * 4, 8) + 4 * k, 8), :] = jnp.where(sub < 4, a, b)
    for q in range(4):
        part = held_ref[pl.ds(base * 4 + q, count, stride=4), :]
        out_ref[pl.ds(base, count), 128 * q : 128 * (q + 1)] = part.astype(BF16)


def spectra_kernel(
    asked_ref, traces_hbm, table_hbm, spectra_hbm, out_hbm,
    traces_ref, table_ref, spectra_ref, rows_ref, held_ref, out_ref, in_sems, table_sem, store_sems, out_sems,
):
    parts = len(range(0, traces_ref.shape[0], STEP))
    table = pltpu.make_async_copy(table_hbm, table_ref, table_sem)
    table.start()
    loads = []
    stores = []
    for b in range(parts):
        at = pl.ds(b * STEP, STEP)
        loads.append(pltpu.make_async_copy(traces_hbm.at[at], traces_ref.at[at], in_sems.at[b]))
        stores.append(
            pltpu.make_async_copy(spectra_ref.at[at], spectra_hbm.at[at], store_sems.at[b])
        )
        loads[b].start()
    table.wait()
    for b in range(parts):
        at = pl.ds(b * STEP, STEP)
        loads[b].wait()
        spectra = jnp.dot(
            traces_ref[at, :], table_ref[...], preferred_element_type=F32
        ).astype(BF16)
        spectra_ref[at, :] = spectra
        put_rows(rows_ref, PAD + b * STEP * 4, spectra.astype(F32))
        stores[b].start()
    peers = asked_ref.shape[0]
    each = peers // GROUPS
    sends = []
    for g in range(GROUPS):

        def one(p, _):
            base = pl.multiple_of(p * DISTINCT, DISTINCT)
            gather_rows(lambda k: asked_ref[p, 0, k], rows_ref, held_ref, out_ref, base, DISTINCT)
            return 0

        lax.fori_loop(g * each, (g + 1) * each, one, 0)
        at = pl.ds(g * each * DISTINCT, each * DISTINCT)
        sends.append(pltpu.make_async_copy(out_ref.at[at], out_hbm.at[at], out_sems.at[g]))
        sends[g].start()
    for copy in stores + sends:
        copy.wait()


def slots_kernel(
    owner_ref, rows_ref, place_ref, src_ref, rcv_ref, taper_ref, key_ref, value_ref, rank_ref
):
    lines, cap = place_ref.shape
    outs = rcv_ref.shape[0]
    rows = rows_ref[...]
    columns = turned(rows)
    places = turned(place_ref[...])
    for g in range(lines):
        same = columns[:, g : g + 1] == rows[g : g + 1, :]
        rank_ref[g : g + 1, :] = jnp.max(
            jnp.where(same, places[:, g : g + 1], -1), axis=0, keepdims=True
        )
    line = lax.broadcasted_iota(jnp.int32, (lines, cap), 0)
    first = jnp.zeros((lines, cap), F32)
    for g in range(lines):
        first = jnp.where(line == g, (owner_ref[g] * DISTINCT).astype(F32), first)
    rank = rank_ref[...].astype(F32).astype(BF16)
    sub = lax.broadcasted_iota(jnp.int32, (cap, cap), 0)

    def some(b, _):
        at = pl.multiple_of(b * 8, 8)
        slots = rcv_ref[pl.ds(at, 8), :]
        rows = []
        for u in range(8):
            slot = slots[u : u + 1, :]
            at_slot = (sub == (slot & (cap - 1))).astype(F32).astype(BF16)
            found = jnp.dot(rank, at_slot, preferred_element_type=F32) + first
            rows.append(
                jnp.sum(jnp.where(line == slot // cap, found, 0.0), axis=0, keepdims=True)
            )
        rows = jnp.concatenate(rows, axis=0).astype(jnp.int32)
        out = lax.broadcasted_iota(jnp.int32, (8, cap), 0) + at
        key_ref[pl.ds(at, 8), :] = (rows * outs + out) * 16 + taper_ref[pl.ds(at, 8), :]
        value_ref[pl.ds(at, 8), :] = src_ref[pl.ds(at, 8), :] * 4
        return 0

    lax.fori_loop(0, outs // 8, some, 0)


def sources_kernel(
    src_ref, spectra_hbm, before_ref, after_ref, out_ref, spectra_ref, all_ref, held_ref, sem
):
    step = pl.program_id(0)

    @pl.when(step == 0)
    def _():
        own = spectra_ref.shape[0]
        copy = pltpu.make_async_copy(spectra_hbm, spectra_ref, sem)
        copy.start()
        put_rows(all_ref, PAD, before_ref[...].astype(F32))
        put_rows(all_ref, PAD + (HALO + own) * 4, after_ref[...].astype(F32))
        copy.wait()

        def one(b, _):
            at = pl.multiple_of(b * TILE, TILE)
            block = spectra_ref[pl.ds(at, TILE), :].astype(F32)
            put_rows(all_ref, PAD + HALO * 4 + at * 4, block)
            return 0

        lax.fori_loop(0, own // TILE, one, 0)

    def one(c, _):
        base = pl.multiple_of(c * 64, 64)
        first = step * out_ref.shape[0] + base
        gather_rows(lambda k: src_ref[first + k], all_ref, held_ref, out_ref, base, 64)
        return 0

    lax.fori_loop(0, out_ref.shape[0] // 64, one, 0)


def pairs_kernel(
    ends_ref, taper_ref, key_ref, source_hbm, arrived_ref, synth_hbm, out_ref,
    source_ref, synth_ref, sum_ref, weight_ref, hot_ref, product_ref, meet_ref, sems, synth_sem,
):
    tiles, _, samples = source_ref.shape
    outs = out_ref.shape[0]
    half = samples // 2
    last = arrived_ref.shape[0] // TILE - 1
    chunk = tiles // CHUNKS

    def load(c):
        at = pl.ds(c * chunk, chunk)
        return pltpu.make_async_copy(source_hbm.at[at], source_ref.at[at], sems.at[c])

    for c in range(CHUNKS):
        load(c).start()
    synth_copy = pltpu.make_async_copy(synth_hbm, synth_ref, synth_sem)
    synth_copy.start()
    meets = meet_ref.shape[0]

    def blank(e, _):
        meet_ref[e] = (meets - tiles) * 64 + tiles - 1
        return 0

    lax.fori_loop(tiles, meets, blank, 0)

    def meet(t, count):
        def add(b, count):
            meet_ref[count] = b * 64 + t
            return count + 1

        return lax.fori_loop(ends_ref[0, t], ends_ref[1, t] + 1, add, count)

    lax.fori_loop(0, tiles, meet, 0)
    entry = key_ref[...] & 15
    weights = jnp.zeros(entry.shape, F32)
    for k in range(taper_ref.shape[0]):
        weights = jnp.where(entry == k, taper_ref[k], weights)
    weight_ref[...] = weights
    sum_ref[...] = jnp.zeros_like(sum_ref)
    sub = lax.broadcasted_iota(jnp.int32, (TILE, TILE), 0)
    out = lax.broadcasted_iota(jnp.int32, (outs, TILE), 0)

    def some(c, _):
        @pl.when(c * UNROLL < tiles)
        def _():
            for u in range(UNROLL // chunk):
                load(c * (UNROLL // chunk) + u).wait()

        for u in range(UNROLL):
            meet = meet_ref[c * UNROLL + u]
            t = meet & 63
            b = meet // 64
            at = pl.multiple_of(jnp.minimum(b, last) * TILE, TILE)
            key = key_ref[pl.ds(t, 1), :]
            row = key // (16 * outs)
            here = jnp.where(row // TILE == b, weight_ref[pl.ds(t, 1), :], 0.0)
            spread = jnp.where(out == ((key // 16) & (outs - 1)), here, 0.0).astype(BF16)
            hot = jnp.where(sub == (row & (TILE - 1)), 1.0, 0.0).astype(BF16)
            right = lax.dot_general(
                hot, arrived_ref[pl.ds(at, TILE), :], (((0,), (0,)), ((), ())),
                preferred_element_type=F32,
            )
            right = right.astype(BF16)
            left = source_ref[t]
            sr, si, rr, ri = left[:, :half], left[:, half:], right[:, :half], right[:, half:]
            product = jnp.concatenate([sr * rr - si * ri, sr * ri + si * rr], axis=1)
            product_ref[u * TILE : (u + 1) * TILE, :] = product
            hot_ref[:, u * TILE : (u + 1) * TILE] = spread
        sum_ref[...] += jnp.dot(hot_ref[...], product_ref[...], preferred_element_type=F32)
        return 0

    lax.fori_loop(0, meet_ref.shape[0] // UNROLL, some, 0)
    synth_copy.wait()
    summed = sum_ref[...].astype(BF16)
    out_ref[...] = jnp.dot(summed, synth_ref[...], preferred_element_type=F32).astype(BF16)


VMEM = pl.BlockSpec(memory_space=pltpu.VMEM)
SMEM = pl.BlockSpec(memory_space=pltpu.SMEM)
HBM = pl.BlockSpec(memory_space=pltpu.HBM)


def shape(dims, kind):
    return jax.ShapeDtypeStruct(dims, kind)


def params(mib):
    return pltpu.CompilerParams(vmem_limit_bytes=mib << 20)


def cost(flops, moved):
    return pl.CostEstimate(flops=flops, bytes_accessed=moved, transcendentals=0)


def body(traces, src_index, rcv_index, taper_index, fetch_rows, line_owner, taper_table):
    sails = lax.axis_size("sail")
    cables = lax.axis_size("cable")
    tr_rows, samples = traces.shape
    outs, aper = src_index.shape
    cap = fetch_rows.shape[1]
    asked, place = pl.pallas_call(
        distinct_kernel,
        in_specs=[SMEM, VMEM],
        out_specs=[VMEM, VMEM],
        out_shape=[shape((sails, 1, cap), jnp.int32), shape((sails, cap), jnp.int32)],
        compiler_params=params(56),
        name="distinct",
    )(line_owner, fetch_rows)
    asked = lax.all_to_all(asked, "sail", split_axis=0, concat_axis=0, tiled=True)
    fetched = sails * DISTINCT
    parts = tr_rows // STEP
    spectra, outgoing = pl.pallas_call(
        spectra_kernel,
        in_specs=[SMEM, HBM, HBM],
        out_specs=[HBM, HBM],
        out_shape=[shape((tr_rows, samples), BF16), shape((fetched, samples), BF16)],
        scratch_shapes=[
            pltpu.VMEM((tr_rows, samples), BF16),
            pltpu.VMEM((samples, samples), BF16),
            pltpu.VMEM((tr_rows, samples), BF16),
            pltpu.VMEM((tr_rows * 4 + 2 * PAD, 128), F32),
            pltpu.VMEM((fetched * 4, 128), F32),
            pltpu.VMEM((fetched, samples), BF16),
            pltpu.SemaphoreType.DMA((parts,)),
            pltpu.SemaphoreType.DMA,
            pltpu.SemaphoreType.DMA((parts,)),
            pltpu.SemaphoreType.DMA((GROUPS,)),
        ],
        compiler_params=params(56),
        name="spectra",
    )(asked, traces, forward_table(samples))
    arrived = lax.all_to_all(
        outgoing.reshape(sails, DISTINCT, samples), "sail", split_axis=0, concat_axis=0, tiled=True
    ).reshape(fetched, samples)
    up = [(i, i + 1) for i in range(cables - 1)]
    before = lax.ppermute(spectra[tr_rows - HALO :], "cable", up)
    after = lax.ppermute(spectra[:HALO], "cable", [(j, i) for i, j in up])
    key, value = pl.pallas_call(
        slots_kernel,
        in_specs=[SMEM] + [VMEM] * 5,
        out_specs=[VMEM, VMEM],
        out_shape=[shape((outs, aper), jnp.int32)] * 2,
        scratch_shapes=[pltpu.VMEM((sails, cap), jnp.int32)],
        compiler_params=params(56),
        name="slots",
        cost_estimate=cost(0, 10 << 20),
    )(line_owner, fetch_rows, place, src_index, rcv_index, taper_index)
    count = outs * aper
    key, value = lax.sort((key.reshape(-1), value.reshape(-1)), num_keys=1, is_stable=False)
    tiles = count // TILE
    blocks = fetched // TILE
    ends = key.reshape(tiles, TILE)[:, :: TILE - 1].T // (16 * outs * TILE)
    meets = -(-(tiles + blocks) // UNROLL) * UNROLL
    sources = pl.pallas_call(
        sources_kernel,
        grid=(8,),
        in_specs=[SMEM, HBM, VMEM, VMEM],
        out_specs=pl.BlockSpec((count // 8, samples), lambda b: (b, 0)),
        out_shape=shape((count, samples), BF16),
        scratch_shapes=[
            pltpu.VMEM((tr_rows, samples), BF16),
            pltpu.VMEM(((tr_rows + 2 * HALO) * 4 + 2 * PAD, 128), F32),
            pltpu.VMEM((count // 8 * 4, 128), F32),
            pltpu.SemaphoreType.DMA,
        ],
        compiler_params=params(56),
        name="sources",
        cost_estimate=cost(0, 40 << 20),
    )(value, spectra, before, after)
    return pl.pallas_call(
        pairs_kernel,
        in_specs=[SMEM, SMEM, VMEM, HBM, VMEM, HBM],
        out_specs=VMEM,
        out_shape=shape((outs, samples), BF16),
        scratch_shapes=[
            pltpu.VMEM((tiles, TILE, samples), BF16),
            pltpu.VMEM((samples, samples), BF16),
            pltpu.VMEM((outs, samples), F32),
            pltpu.VMEM((tiles, TILE), F32),
            pltpu.VMEM((outs, UNROLL * TILE), BF16),
            pltpu.VMEM((UNROLL * TILE, samples), BF16),
            pltpu.SMEM((meets,), jnp.int32),
            pltpu.SemaphoreType.DMA((CHUNKS,)),
            pltpu.SemaphoreType.DMA,
        ],
        compiler_params=params(50),
        name="pairs",
    )(
        ends, taper_table, key.reshape(tiles, TILE), sources.reshape(tiles, TILE, samples), arrived,
        synthesis_table(samples, aper),
    )


def solution(mesh):
    split = P(("sail", "cable"), None)
    return jax.shard_map(
        body,
        mesh=mesh,
        in_specs=(split, split, split, split, split, P(), P()),
        out_specs=split,
        check_vma=False,
    )
```

```python
import math

import jax
import jax.numpy as jnp
import ml_dtypes
import numpy as np
from jax import lax
from jax.experimental import pallas as pl
from jax.experimental.pallas import tpu as pltpu
from jax.sharding import PartitionSpec as P

HALO = 64
DISTINCT = 64
PAD = 8
TILE = 256
STEP = 512
GROUPS = 4
CHUNKS = 8
UNROLL = 8
F32 = jnp.float32
BF16 = jnp.bfloat16


def forward_table(samples):
    turns = np.arange(samples)[:, None] * np.arange(samples // 2)[None, :] % samples
    angle = turns * (2.0 * math.pi / samples)
    table = np.concatenate([np.cos(angle), -np.sin(angle)], axis=1) / math.sqrt(samples)
    return jnp.asarray(table.astype(np.float32).astype(ml_dtypes.bfloat16))


def synthesis_table(samples, aperture):
    turns = np.arange(samples // 2)[:, None] * np.arange(samples)[None, :] % samples
    angle = turns * (2.0 * math.pi / samples)
    scale = math.sqrt(aperture * (samples // 2))
    table = np.concatenate([np.cos(angle), -np.sin(angle)], axis=0) / scale
    return jnp.asarray(table.astype(np.float32).astype(ml_dtypes.bfloat16))


def turned(values):
    lines, cap = values.shape
    return jnp.concatenate([values, jnp.zeros((cap - lines, cap), values.dtype)], axis=0).T


def order_kernel(owner_ref, rows_hbm, out_hbm, sems):
    copies = []
    for g in range(rows_hbm.shape[0]):
        copies.append(
            pltpu.make_async_copy(rows_hbm.at[g], out_hbm.at[owner_ref[g]], sems.at[g])
        )
        copies[g].start()
    for copy in copies:
        copy.wait()


def first_entries(rows):
    lines, cap = rows.shape
    sub = lax.broadcasted_iota(jnp.int32, (cap, cap), 0)
    lane = lax.broadcasted_iota(jnp.int32, (cap, cap), 1)
    earlier = sub < lane
    columns = turned(rows)
    repeats = []
    for g in range(lines):
        same = (columns[:, g : g + 1] == rows[g : g + 1, :]) & earlier
        repeats.append(jnp.max(jnp.where(same, 1.0, 0.0), axis=0, keepdims=True))
    once = 1.0 - jnp.concatenate(repeats, axis=0)
    before = jnp.where(earlier, 1.0, 0.0).astype(BF16)
    place = jnp.dot(once.astype(BF16), before, preferred_element_type=F32)
    return columns, jnp.where(once > 0.0, place, -1.0).astype(jnp.int32)


def put_rows(ref, start, block):
    for q in range(4):
        at = pl.ds(start + q, block.shape[0], stride=4)
        ref[at, :] = block[:, 128 * q : 128 * (q + 1)]


def gather_rows(index, rows_ref, held_ref, out_ref, base, count):
    sub = lax.broadcasted_iota(jnp.int32, (8, 128), 0)
    for k in range(0, count, 2):
        a = rows_ref[pl.ds(index(k) + PAD, 8), :]
        b = rows_ref[pl.ds(index(k + 1) + PAD - 4, 8), :]
        held_ref[pl.ds(pl.multiple_of(base * 4, 8) + 4 * k, 8), :] = jnp.where(sub < 4, a, b)
    for q in range(4):
        part = held_ref[pl.ds(base * 4 + q, count, stride=4), :]
        out_ref[pl.ds(base, count), 128 * q : 128 * (q + 1)] = part.astype(BF16)


def spectra_kernel(
    lists_ref, traces_hbm, table_hbm, spectra_hbm, out_hbm,
    traces_ref, table_ref, spectra_ref, rows_ref, held_ref, out_ref, distinct_ref, asked_ref,
    in_sems, table_sem, asked_sem, store_sems, out_sems,
):
    parts = len(range(0, traces_ref.shape[0], STEP))
    table = pltpu.make_async_copy(table_hbm, table_ref, table_sem)
    table.start()
    loads = []
    stores = []
    for b in range(parts):
        at = pl.ds(b * STEP, STEP)
        loads.append(pltpu.make_async_copy(traces_hbm.at[at], traces_ref.at[at], in_sems.at[b]))
        stores.append(
            pltpu.make_async_copy(spectra_ref.at[at], spectra_hbm.at[at], store_sems.at[b])
        )
        loads[b].start()
    lists = lists_ref[...]
    columns, place = first_entries(lists)
    places = turned(place)
    lane = lax.broadcasted_iota(jnp.int32, columns.shape, 1)
    for g in range(lists.shape[0]):
        match = places[:, g : g + 1] == lane
        picked = jnp.max(jnp.where(match, columns[:, g : g + 1], 0), axis=0, keepdims=True)
        distinct_ref[g : g + 1, :] = picked * 4
    asking = pltpu.make_async_copy(distinct_ref, asked_ref, asked_sem)
    asking.start()
    table.wait()
    for b in range(parts):
        at = pl.ds(b * STEP, STEP)
        loads[b].wait()
        spectra = jnp.dot(
            traces_ref[at, :], table_ref[...], preferred_element_type=F32
        ).astype(BF16)
        spectra_ref[at, :] = spectra
        put_rows(rows_ref, PAD + b * STEP * 4, spectra.astype(F32))
        stores[b].start()
    asking.wait()
    peers = asked_ref.shape[0]
    each = peers // GROUPS
    sends = []
    for g in range(GROUPS):

        def one(p, _):
            base = pl.multiple_of(p * DISTINCT, DISTINCT)
            gather_rows(lambda k: asked_ref[p, k], rows_ref, held_ref, out_ref, base, DISTINCT)
            return 0

        lax.fori_loop(g * each, (g + 1) * each, one, 0)
        at = pl.ds(g * each * DISTINCT, each * DISTINCT)
        sends.append(pltpu.make_async_copy(out_ref.at[at], out_hbm.at[at], out_sems.at[g]))
        sends[g].start()
    for copy in stores + sends:
        copy.wait()


def slots_kernel(
    owner_ref, rows_ref, src_ref, rcv_ref, taper_ref, key_ref, value_ref, rank_ref
):
    lines, cap = rows_ref.shape
    outs = rcv_ref.shape[0]
    rows = rows_ref[...]
    columns, place = first_entries(rows)
    places = turned(place)
    for g in range(lines):
        same = columns[:, g : g + 1] == rows[g : g + 1, :]
        rank_ref[g : g + 1, :] = jnp.max(
            jnp.where(same, places[:, g : g + 1], -1), axis=0, keepdims=True
        )
    line = lax.broadcasted_iota(jnp.int32, (lines, cap), 0)
    first = jnp.zeros((lines, cap), F32)
    for g in range(lines):
        first = jnp.where(line == g, (owner_ref[g] * DISTINCT).astype(F32), first)
    rank = rank_ref[...].astype(F32).astype(BF16)
    sub = lax.broadcasted_iota(jnp.int32, (cap, cap), 0)

    def some(b, _):
        at = pl.multiple_of(b * 8, 8)
        slots = rcv_ref[pl.ds(at, 8), :]
        rows = []
        for u in range(8):
            slot = slots[u : u + 1, :]
            at_slot = (sub == (slot & (cap - 1))).astype(F32).astype(BF16)
            found = jnp.dot(rank, at_slot, preferred_element_type=F32) + first
            rows.append(
                jnp.sum(jnp.where(line == slot // cap, found, 0.0), axis=0, keepdims=True)
            )
        rows = jnp.concatenate(rows, axis=0).astype(jnp.int32)
        out = lax.broadcasted_iota(jnp.int32, (8, cap), 0) + at
        key_ref[pl.ds(at, 8), :] = (rows * outs + out) * 16 + taper_ref[pl.ds(at, 8), :]
        value_ref[pl.ds(at, 8), :] = src_ref[pl.ds(at, 8), :] * 4
        return 0

    lax.fori_loop(0, outs // 8, some, 0)


def sources_kernel(
    src_ref, spectra_hbm, before_ref, after_ref, out_ref, spectra_ref, all_ref, held_ref, sem
):
    step = pl.program_id(0)

    @pl.when(step == 0)
    def _():
        own = spectra_ref.shape[0]
        copy = pltpu.make_async_copy(spectra_hbm, spectra_ref, sem)
        copy.start()
        put_rows(all_ref, PAD, before_ref[...].astype(F32))
        put_rows(all_ref, PAD + (HALO + own) * 4, after_ref[...].astype(F32))
        copy.wait()

        def one(b, _):
            at = pl.multiple_of(b * TILE, TILE)
            block = spectra_ref[pl.ds(at, TILE), :].astype(F32)
            put_rows(all_ref, PAD + HALO * 4 + at * 4, block)
            return 0

        lax.fori_loop(0, own // TILE, one, 0)

    def one(c, _):
        base = pl.multiple_of(c * 64, 64)
        first = step * out_ref.shape[0] + base
        gather_rows(lambda k: src_ref[first + k], all_ref, held_ref, out_ref, base, 64)
        return 0

    lax.fori_loop(0, out_ref.shape[0] // 64, one, 0)


def pairs_kernel(
    ends_ref, taper_ref, key_ref, source_hbm, arrived_ref, synth_hbm, out_ref,
    source_ref, synth_ref, sum_ref, weight_ref, hot_ref, product_ref, meet_ref, sems, synth_sem,
):
    tiles, _, samples = source_ref.shape
    outs = out_ref.shape[0]
    half = samples // 2
    last = arrived_ref.shape[0] // TILE - 1
    chunk = tiles // CHUNKS

    def load(c):
        at = pl.ds(c * chunk, chunk)
        return pltpu.make_async_copy(source_hbm.at[at], source_ref.at[at], sems.at[c])

    for c in range(CHUNKS):
        load(c).start()
    synth_copy = pltpu.make_async_copy(synth_hbm, synth_ref, synth_sem)
    synth_copy.start()
    meets = meet_ref.shape[0]

    def blank(e, _):
        meet_ref[e] = (meets - tiles) * 64 + tiles - 1
        return 0

    lax.fori_loop(tiles, meets, blank, 0)

    def meet(t, count):
        def add(b, count):
            meet_ref[count] = b * 64 + t
            return count + 1

        return lax.fori_loop(ends_ref[0, t], ends_ref[1, t] + 1, add, count)

    lax.fori_loop(0, tiles, meet, 0)
    entry = key_ref[...] & 15
    weights = jnp.zeros(entry.shape, F32)
    for k in range(taper_ref.shape[0]):
        weights = jnp.where(entry == k, taper_ref[k], weights)
    weight_ref[...] = weights
    sum_ref[...] = jnp.zeros_like(sum_ref)
    sub = lax.broadcasted_iota(jnp.int32, (TILE, TILE), 0)
    out = lax.broadcasted_iota(jnp.int32, (outs, TILE), 0)

    def some(c, _):
        @pl.when(c * UNROLL < tiles)
        def _():
            for u in range(UNROLL // chunk):
                load(c * (UNROLL // chunk) + u).wait()

        for u in range(UNROLL):
            meet = meet_ref[c * UNROLL + u]
            t = meet & 63
            b = meet // 64
            at = pl.multiple_of(jnp.minimum(b, last) * TILE, TILE)
            key = key_ref[pl.ds(t, 1), :]
            row = key // (16 * outs)
            here = jnp.where(row // TILE == b, weight_ref[pl.ds(t, 1), :], 0.0)
            spread = jnp.where(out == ((key // 16) & (outs - 1)), here, 0.0).astype(BF16)
            hot = jnp.where(sub == (row & (TILE - 1)), 1.0, 0.0).astype(BF16)
            right = lax.dot_general(
                hot, arrived_ref[pl.ds(at, TILE), :], (((0,), (0,)), ((), ())),
                preferred_element_type=F32,
            )
            right = right.astype(BF16)
            left = source_ref[t]
            sr, si, rr, ri = left[:, :half], left[:, half:], right[:, :half], right[:, half:]
            product = jnp.concatenate([sr * rr - si * ri, sr * ri + si * rr], axis=1)
            product_ref[u * TILE : (u + 1) * TILE, :] = product
            hot_ref[:, u * TILE : (u + 1) * TILE] = spread
        sum_ref[...] += jnp.dot(hot_ref[...], product_ref[...], preferred_element_type=F32)
        return 0

    lax.fori_loop(0, meet_ref.shape[0] // UNROLL, some, 0)
    synth_copy.wait()
    summed = sum_ref[...].astype(BF16)
    out_ref[...] = jnp.dot(summed, synth_ref[...], preferred_element_type=F32).astype(BF16)


VMEM = pl.BlockSpec(memory_space=pltpu.VMEM)
SMEM = pl.BlockSpec(memory_space=pltpu.SMEM)
HBM = pl.BlockSpec(memory_space=pltpu.HBM)


def shape(dims, kind):
    return jax.ShapeDtypeStruct(dims, kind)


def params(mib):
    return pltpu.CompilerParams(vmem_limit_bytes=mib << 20)


def cost(flops, moved):
    return pl.CostEstimate(flops=flops, bytes_accessed=moved, transcendentals=0)


def body(traces, src_index, rcv_index, taper_index, fetch_rows, line_owner, taper_table):
    sails = lax.axis_size("sail")
    cables = lax.axis_size("cable")
    tr_rows, samples = traces.shape
    outs, aper = src_index.shape
    cap = fetch_rows.shape[1]
    lists = pl.pallas_call(
        order_kernel,
        in_specs=[SMEM, HBM],
        out_specs=HBM,
        out_shape=shape((sails, 1, cap), jnp.int32),
        scratch_shapes=[pltpu.SemaphoreType.DMA((sails,))],
        compiler_params=params(56),
        name="order",
    )(line_owner, fetch_rows.reshape(sails, 1, cap))
    lists = lax.all_to_all(lists, "sail", split_axis=0, concat_axis=0, tiled=True)
    fetched = sails * DISTINCT
    parts = tr_rows // STEP
    spectra, outgoing = pl.pallas_call(
        spectra_kernel,
        in_specs=[VMEM, HBM, HBM],
        out_specs=[HBM, HBM],
        out_shape=[shape((tr_rows, samples), BF16), shape((fetched, samples), BF16)],
        scratch_shapes=[
            pltpu.VMEM((tr_rows, samples), BF16),
            pltpu.VMEM((samples, samples), BF16),
            pltpu.VMEM((tr_rows, samples), BF16),
            pltpu.VMEM((tr_rows * 4 + 2 * PAD, 128), F32),
            pltpu.VMEM((fetched * 4, 128), F32),
            pltpu.VMEM((fetched, samples), BF16),
            pltpu.VMEM((sails, cap), jnp.int32),
            pltpu.SMEM((sails, cap), jnp.int32),
            pltpu.SemaphoreType.DMA((parts,)),
            pltpu.SemaphoreType.DMA,
            pltpu.SemaphoreType.DMA,
            pltpu.SemaphoreType.DMA((parts,)),
            pltpu.SemaphoreType.DMA((GROUPS,)),
        ],
        compiler_params=params(56),
        name="spectra",
    )(lists.reshape(sails, cap), traces, forward_table(samples))
    arrived = lax.all_to_all(
        outgoing.reshape(sails, DISTINCT, samples), "sail", split_axis=0, concat_axis=0, tiled=True
    ).reshape(fetched, samples)
    up = [(i, i + 1) for i in range(cables - 1)]
    before = lax.ppermute(spectra[tr_rows - HALO :], "cable", up)
    after = lax.ppermute(spectra[:HALO], "cable", [(j, i) for i, j in up])
    key, value = pl.pallas_call(
        slots_kernel,
        in_specs=[SMEM] + [VMEM] * 4,
        out_specs=[VMEM, VMEM],
        out_shape=[shape((outs, aper), jnp.int32)] * 2,
        scratch_shapes=[pltpu.VMEM((sails, cap), jnp.int32)],
        compiler_params=params(56),
        name="slots",
        cost_estimate=cost(0, 10 << 20),
    )(line_owner, fetch_rows, src_index, rcv_index, taper_index)
    count = outs * aper
    key, value = lax.sort((key.reshape(-1), value.reshape(-1)), num_keys=1, is_stable=False)
    tiles = count // TILE
    blocks = fetched // TILE
    ends = key.reshape(tiles, TILE)[:, :: TILE - 1].T // (16 * outs * TILE)
    meets = -(-(tiles + blocks) // UNROLL) * UNROLL
    sources = pl.pallas_call(
        sources_kernel,
        grid=(8,),
        in_specs=[SMEM, HBM, VMEM, VMEM],
        out_specs=pl.BlockSpec((count // 8, samples), lambda b: (b, 0)),
        out_shape=shape((count, samples), BF16),
        scratch_shapes=[
            pltpu.VMEM((tr_rows, samples), BF16),
            pltpu.VMEM(((tr_rows + 2 * HALO) * 4 + 2 * PAD, 128), F32),
            pltpu.VMEM((count // 8 * 4, 128), F32),
            pltpu.SemaphoreType.DMA,
        ],
        compiler_params=params(56),
        name="sources",
        cost_estimate=cost(0, 40 << 20),
    )(value, spectra, before, after)
    return pl.pallas_call(
        pairs_kernel,
        in_specs=[SMEM, SMEM, VMEM, HBM, VMEM, HBM],
        out_specs=VMEM,
        out_shape=shape((outs, samples), BF16),
        scratch_shapes=[
            pltpu.VMEM((tiles, TILE, samples), BF16),
            pltpu.VMEM((samples, samples), BF16),
            pltpu.VMEM((outs, samples), F32),
            pltpu.VMEM((tiles, TILE), F32),
            pltpu.VMEM((outs, UNROLL * TILE), BF16),
            pltpu.VMEM((UNROLL * TILE, samples), BF16),
            pltpu.SMEM((meets,), jnp.int32),
            pltpu.SemaphoreType.DMA((CHUNKS,)),
            pltpu.SemaphoreType.DMA,
        ],
        compiler_params=params(50),
        name="pairs",
    )(
        ends, taper_table, key.reshape(tiles, TILE), sources.reshape(tiles, TILE, samples), arrived,
        synthesis_table(samples, aper),
    )


def solution(mesh):
    split = P(("sail", "cable"), None)
    return jax.shard_map(
        body,
        mesh=mesh,
        in_specs=(split, split, split, split, split, P(), P()),
        out_specs=split,
        check_vma=False,
    )
```

```python
import math

import jax
import jax.numpy as jnp
import ml_dtypes
import numpy as np
from jax import lax
from jax.experimental import pallas as pl
from jax.experimental.pallas import tpu as pltpu
from jax.sharding import PartitionSpec as P

HALO = 64
DISTINCT = 64
PAD = 8
TILE = 256
STEP = 512
GROUPS = 4
CHUNKS = 8
UNROLL = 8
HEAD = 4
F32 = jnp.float32
BF16 = jnp.bfloat16


def forward_table(samples):
    turns = np.arange(samples)[:, None] * np.arange(samples // 2)[None, :] % samples
    angle = turns * (2.0 * math.pi / samples)
    table = np.concatenate([np.cos(angle), -np.sin(angle)], axis=1) / math.sqrt(samples)
    return jnp.asarray(table.astype(np.float32).astype(ml_dtypes.bfloat16))


def synthesis_table(samples, aperture):
    turns = np.arange(samples // 2)[:, None] * np.arange(samples)[None, :] % samples
    angle = turns * (2.0 * math.pi / samples)
    scale = math.sqrt(aperture * (samples // 2))
    table = np.concatenate([np.cos(angle), -np.sin(angle)], axis=0) / scale
    return jnp.asarray(table.astype(np.float32).astype(ml_dtypes.bfloat16))


def turned(values):
    lines, cap = values.shape
    return jnp.concatenate([values, jnp.zeros((cap - lines, cap), values.dtype)], axis=0).T


def order_kernel(owner_ref, rows_ref, out_ref):
    for g in range(rows_ref.shape[0]):
        out_ref[owner_ref[g]] = rows_ref[g : g + 1, :]


def first_entries(rows):
    lines, cap = rows.shape
    sub = lax.broadcasted_iota(jnp.int32, (cap, cap), 0)
    lane = lax.broadcasted_iota(jnp.int32, (cap, cap), 1)
    earlier = sub < lane
    columns = turned(rows)
    repeats = []
    for g in range(lines):
        same = (columns[:, g : g + 1] == rows[g : g + 1, :]) & earlier
        repeats.append(jnp.max(jnp.where(same, 1.0, 0.0), axis=0, keepdims=True))
    once = 1.0 - jnp.concatenate(repeats, axis=0)
    before = jnp.where(earlier, 1.0, 0.0).astype(BF16)
    place = jnp.dot(once.astype(BF16), before, preferred_element_type=F32)
    return columns, jnp.where(once > 0.0, place, -1.0).astype(jnp.int32)


def put_rows(ref, start, block):
    for q in range(4):
        at = pl.ds(start + q, block.shape[0], stride=4)
        ref[at, :] = block[:, 128 * q : 128 * (q + 1)]


def gather_rows(index, rows_ref, held_ref, out_ref, base, count):
    sub = lax.broadcasted_iota(jnp.int32, (8, 128), 0)
    for k in range(0, count, 2):
        a = rows_ref[pl.ds(index(k) + PAD, 8), :]
        b = rows_ref[pl.ds(index(k + 1) + PAD - 4, 8), :]
        held_ref[pl.ds(pl.multiple_of(base * 4, 8) + 4 * k, 8), :] = jnp.where(sub < 4, a, b)
    for q in range(4):
        part = held_ref[pl.ds(base * 4 + q, count, stride=4), :]
        out_ref[pl.ds(base, count), 128 * q : 128 * (q + 1)] = part.astype(BF16)


def spectra_kernel(
    lists_ref, traces_hbm, table_hbm, first_hbm, last_hbm, out_hbm,
    traces_ref, table_ref, edge_ref, rows_ref, held_ref, out_ref, distinct_ref, asked_ref,
    in_sems, table_sem, asked_sem, edge_sems, out_sems,
):
    parts = len(range(0, traces_ref.shape[0], STEP))
    table = pltpu.make_async_copy(table_hbm, table_ref, table_sem)
    table.start()
    loads = []
    stores = []
    for b in range(parts):
        at = pl.ds(b * STEP, STEP)
        loads.append(pltpu.make_async_copy(traces_hbm.at[at], traces_ref.at[at], in_sems.at[b]))
        loads[b].start()
    lists = lists_ref[...]
    columns, place = first_entries(lists)
    places = turned(place)
    lane = lax.broadcasted_iota(jnp.int32, columns.shape, 1)
    for g in range(lists.shape[0]):
        match = places[:, g : g + 1] == lane
        picked = jnp.max(jnp.where(match, columns[:, g : g + 1], 0), axis=0, keepdims=True)
        distinct_ref[g : g + 1, :] = picked * 4
    asking = pltpu.make_async_copy(distinct_ref, asked_ref, asked_sem)
    asking.start()
    table.wait()
    for b in range(parts):
        at = pl.ds(b * STEP, STEP)
        loads[b].wait()
        spectra = jnp.dot(
            traces_ref[at, :], table_ref[...], preferred_element_type=F32
        ).astype(BF16)
        put_rows(rows_ref, PAD + b * STEP * 4, spectra.astype(F32))
        for edge, hbm, part, first in ((0, first_hbm, 0, 0), (1, last_hbm, parts - 1, STEP - HALO)):
            if b == part:
                edge_ref[edge] = spectra[first : first + HALO]
                stores.append(pltpu.make_async_copy(edge_ref.at[edge], hbm, edge_sems.at[edge]))
                stores[edge].start()
    asking.wait()
    peers = asked_ref.shape[0]
    each = peers // GROUPS
    sends = []
    for g in range(GROUPS):

        def one(p, _):
            base = pl.multiple_of(p * DISTINCT, DISTINCT)
            gather_rows(lambda k: asked_ref[p, k], rows_ref, held_ref, out_ref, base, DISTINCT)
            return 0

        lax.fori_loop(g * each, (g + 1) * each, one, 0)
        at = pl.ds(g * each * DISTINCT, each * DISTINCT)
        sends.append(pltpu.make_async_copy(out_ref.at[at], out_hbm.at[at], out_sems.at[g]))
        sends[g].start()
    for copy in stores + sends:
        copy.wait()


def slots_kernel(
    owner_ref, rows_ref, src_ref, rcv_ref, taper_ref, key_ref, value_ref, rank_ref
):
    lines, cap = rows_ref.shape
    outs = rcv_ref.shape[0]
    rows = rows_ref[...]
    columns, place = first_entries(rows)
    places = turned(place)
    for g in range(lines):
        same = columns[:, g : g + 1] == rows[g : g + 1, :]
        rank_ref[g : g + 1, :] = jnp.max(
            jnp.where(same, places[:, g : g + 1], -1), axis=0, keepdims=True
        )
    line = lax.broadcasted_iota(jnp.int32, (lines, cap), 0)
    first = jnp.zeros((lines, cap), F32)
    for g in range(lines):
        first = jnp.where(line == g, (owner_ref[g] * DISTINCT).astype(F32), first)
    rank = rank_ref[...].astype(F32).astype(BF16)
    sub = lax.broadcasted_iota(jnp.int32, (cap, cap), 0)

    def some(b, _):
        at = pl.multiple_of(b * 8, 8)
        slots = rcv_ref[pl.ds(at, 8), :]
        rows = []
        for u in range(8):
            slot = slots[u : u + 1, :]
            at_slot = (sub == (slot & (cap - 1))).astype(F32).astype(BF16)
            found = jnp.dot(rank, at_slot, preferred_element_type=F32) + first
            rows.append(
                jnp.sum(jnp.where(line == slot // cap, found, 0.0), axis=0, keepdims=True)
            )
        rows = jnp.concatenate(rows, axis=0).astype(jnp.int32)
        out = lax.broadcasted_iota(jnp.int32, (8, cap), 0) + at
        key_ref[pl.ds(at, 8), :] = (rows * outs + out) * 16 + taper_ref[pl.ds(at, 8), :]
        value_ref[pl.ds(at, 8), :] = src_ref[pl.ds(at, 8), :] * 4
        return 0

    lax.fori_loop(0, outs // 8, some, 0)


def sources_kernel(
    src_ref, traces_hbm, table_hbm, before_ref, after_ref, out_ref,
    traces_ref, table_ref, all_ref, held_ref, sems,
):
    step = pl.program_id(0)

    @pl.when(step == 0)
    def _():
        own = traces_ref.shape[0]
        copies = [
            pltpu.make_async_copy(traces_hbm, traces_ref, sems.at[0]),
            pltpu.make_async_copy(table_hbm, table_ref, sems.at[1]),
        ]
        for copy in copies:
            copy.start()
        put_rows(all_ref, PAD, before_ref[...].astype(F32))
        put_rows(all_ref, PAD + (HALO + own) * 4, after_ref[...].astype(F32))
        for copy in copies:
            copy.wait()

        def one(b, _):
            at = pl.multiple_of(b * STEP, STEP)
            spectra = jnp.dot(
                traces_ref[pl.ds(at, STEP), :], table_ref[...], preferred_element_type=F32
            ).astype(BF16)
            put_rows(all_ref, PAD + HALO * 4 + at * 4, spectra.astype(F32))
            return 0

        lax.fori_loop(0, own // STEP, one, 0)

    def one(c, _):
        base = pl.multiple_of(c * 64, 64)
        first = step * out_ref.shape[0] + base
        gather_rows(lambda k: src_ref[first + k], all_ref, held_ref, out_ref, base, 64)
        return 0

    lax.fori_loop(0, out_ref.shape[0] // 64, one, 0)


def pairs_kernel(
    ends_ref, taper_ref, key_ref, source_hbm, arrived_ref, synth_hbm, out_ref,
    source_ref, synth_ref, sum_ref, weight_ref, hot_ref, product_ref, meet_ref, sems, synth_sem,
):
    tiles, _, samples = source_ref.shape
    outs = out_ref.shape[0]
    half = samples // 2
    last = arrived_ref.shape[0] // TILE - 1
    chunk = tiles // CHUNKS

    def load(c):
        at = pl.ds(c * chunk, chunk)
        return pltpu.make_async_copy(source_hbm.at[at], source_ref.at[at], sems.at[c])

    for c in range(CHUNKS):
        load(c).start()
    synth_copy = pltpu.make_async_copy(synth_hbm, synth_ref, synth_sem)
    synth_copy.start()
    meets = meet_ref.shape[0]

    def blank(e, _):
        meet_ref[e] = (meets - tiles) * 64 + tiles - 1
        return 0

    lax.fori_loop(tiles, meets, blank, 0)

    def meet(t, count):
        def add(b, count):
            meet_ref[count] = b * 64 + t
            return count + 1

        return lax.fori_loop(ends_ref[0, t], ends_ref[1, t] + 1, add, count)

    lax.fori_loop(0, tiles, meet, 0)
    entry = key_ref[...] & 15
    weights = jnp.zeros(entry.shape, F32)
    for k in range(taper_ref.shape[0]):
        weights = jnp.where(entry == k, taper_ref[k], weights)
    weight_ref[...] = weights
    sum_ref[...] = jnp.zeros_like(sum_ref)
    sub = lax.broadcasted_iota(jnp.int32, (TILE, TILE), 0)
    out = lax.broadcasted_iota(jnp.int32, (outs, TILE), 0)

    def some(base, count):
        for u in range(count):
            meet = meet_ref[base + u]
            t = meet & 63
            b = meet // 64
            at = pl.multiple_of(jnp.minimum(b, last) * TILE, TILE)
            key = key_ref[pl.ds(t, 1), :]
            row = key // (16 * outs)
            here = jnp.where(row // TILE == b, weight_ref[pl.ds(t, 1), :], 0.0)
            spread = jnp.where(out == ((key // 16) & (outs - 1)), here, 0.0).astype(BF16)
            hot = jnp.where(sub == (row & (TILE - 1)), 1.0, 0.0).astype(BF16)
            right = lax.dot_general(
                hot, arrived_ref[pl.ds(at, TILE), :], (((0,), (0,)), ((), ())),
                preferred_element_type=F32,
            ).astype(BF16)
            left = source_ref[t]
            sr, si, rr, ri = left[:, :half], left[:, half:], right[:, :half], right[:, half:]
            product = jnp.concatenate([sr * rr - si * ri, sr * ri + si * rr], axis=1)
            product_ref[u * TILE : (u + 1) * TILE, :] = product
            hot_ref[:, u * TILE : (u + 1) * TILE] = spread
        width = count * TILE
        sum_ref[...] += jnp.dot(
            hot_ref[:, :width], product_ref[:width, :], preferred_element_type=F32
        )

    load(0).wait()
    some(0, HEAD)

    def later(c, _):
        base = HEAD + c * UNROLL

        @pl.when(base < tiles)
        def _():
            for u in range(UNROLL // chunk):
                part = base // chunk + u

                @pl.when(part < CHUNKS)
                def _():
                    load(part).wait()

        some(base, UNROLL)
        return 0

    rest = (meets - HEAD) % UNROLL
    lax.fori_loop(0, (meets - HEAD) // UNROLL, later, 0)
    if rest:
        some(meets - rest, rest)
    synth_copy.wait()
    summed = sum_ref[...].astype(BF16)
    out_ref[...] = jnp.dot(summed, synth_ref[...], preferred_element_type=F32).astype(BF16)


VMEM = pl.BlockSpec(memory_space=pltpu.VMEM)
SMEM = pl.BlockSpec(memory_space=pltpu.SMEM)
HBM = pl.BlockSpec(memory_space=pltpu.HBM)


def shape(dims, kind):
    return jax.ShapeDtypeStruct(dims, kind)


def params(mib):
    return pltpu.CompilerParams(vmem_limit_bytes=mib << 20)


def cost(flops, moved):
    return pl.CostEstimate(flops=flops, bytes_accessed=moved, transcendentals=0)


def body(traces, src_index, rcv_index, taper_index, fetch_rows, line_owner, taper_table):
    sails = lax.axis_size("sail")
    cables = lax.axis_size("cable")
    tr_rows, samples = traces.shape
    outs, aper = src_index.shape
    cap = fetch_rows.shape[1]
    lists = pl.pallas_call(
        order_kernel,
        in_specs=[SMEM, VMEM],
        out_specs=VMEM,
        out_shape=shape((sails, 1, cap), jnp.int32),
        compiler_params=params(56),
        name="order",
    )(line_owner, fetch_rows)
    lists = lax.all_to_all(lists, "sail", split_axis=0, concat_axis=0, tiled=True)
    fetched = sails * DISTINCT
    parts = tr_rows // STEP
    table = forward_table(samples)
    first, last, outgoing = pl.pallas_call(
        spectra_kernel,
        in_specs=[VMEM, HBM, HBM],
        out_specs=[HBM, HBM, HBM],
        out_shape=[
            shape((HALO, samples), BF16),
            shape((HALO, samples), BF16),
            shape((fetched, samples), BF16),
        ],
        scratch_shapes=[
            pltpu.VMEM((tr_rows, samples), BF16),
            pltpu.VMEM((samples, samples), BF16),
            pltpu.VMEM((2, HALO, samples), BF16),
            pltpu.VMEM((tr_rows * 4 + 2 * PAD, 128), F32),
            pltpu.VMEM((fetched * 4, 128), F32),
            pltpu.VMEM((fetched, samples), BF16),
            pltpu.VMEM((sails, cap), jnp.int32),
            pltpu.SMEM((sails, cap), jnp.int32),
            pltpu.SemaphoreType.DMA((parts,)),
            pltpu.SemaphoreType.DMA,
            pltpu.SemaphoreType.DMA,
            pltpu.SemaphoreType.DMA((2,)),
            pltpu.SemaphoreType.DMA((GROUPS,)),
        ],
        compiler_params=params(56),
        name="spectra",
    )(lists.reshape(sails, cap), traces, table)
    arrived = lax.all_to_all(
        outgoing.reshape(sails, DISTINCT, samples), "sail", split_axis=0, concat_axis=0, tiled=True
    ).reshape(fetched, samples)
    up = [(i, i + 1) for i in range(cables - 1)]
    before = lax.ppermute(last, "cable", up)
    after = lax.ppermute(first, "cable", [(j, i) for i, j in up])
    key, value = pl.pallas_call(
        slots_kernel,
        in_specs=[SMEM] + [VMEM] * 4,
        out_specs=[VMEM, VMEM],
        out_shape=[shape((outs, aper), jnp.int32)] * 2,
        scratch_shapes=[pltpu.VMEM((sails, cap), jnp.int32)],
        compiler_params=params(56),
        name="slots",
        cost_estimate=cost(0, 10 << 20),
    )(line_owner, fetch_rows, src_index, rcv_index, taper_index)
    count = outs * aper
    key, value = lax.sort((key.reshape(-1), value.reshape(-1)), num_keys=1, is_stable=False)
    tiles = count // TILE
    blocks = fetched // TILE
    ends = key.reshape(tiles, TILE)[:, :: TILE - 1].T // (16 * outs * TILE)
    meets = -(-(tiles + blocks) // HEAD) * HEAD
    sources = pl.pallas_call(
        sources_kernel,
        grid=(8,),
        in_specs=[SMEM, HBM, HBM, VMEM, VMEM],
        out_specs=pl.BlockSpec((count // 8, samples), lambda b: (b, 0)),
        out_shape=shape((count, samples), BF16),
        scratch_shapes=[
            pltpu.VMEM((tr_rows, samples), BF16),
            pltpu.VMEM((samples, samples), BF16),
            pltpu.VMEM(((tr_rows + 2 * HALO) * 4 + 2 * PAD, 128), F32),
            pltpu.VMEM((count // 8 * 4, 128), F32),
            pltpu.SemaphoreType.DMA((2,)),
        ],
        compiler_params=params(56),
        name="sources",
        cost_estimate=cost(0, 40 << 20),
    )(value, traces, table, before, after)
    return pl.pallas_call(
        pairs_kernel,
        in_specs=[SMEM, SMEM, VMEM, HBM, VMEM, HBM],
        out_specs=VMEM,
        out_shape=shape((outs, samples), BF16),
        scratch_shapes=[
            pltpu.VMEM((tiles, TILE, samples), BF16),
            pltpu.VMEM((samples, samples), BF16),
            pltpu.VMEM((outs, samples), F32),
            pltpu.VMEM((tiles, TILE), F32),
            pltpu.VMEM((outs, UNROLL * TILE), BF16),
            pltpu.VMEM((UNROLL * TILE, samples), BF16),
            pltpu.SMEM((meets,), jnp.int32),
            pltpu.SemaphoreType.DMA((CHUNKS,)),
            pltpu.SemaphoreType.DMA,
        ],
        compiler_params=params(50),
        name="pairs",
    )(
        ends, taper_table, key.reshape(tiles, TILE), sources.reshape(tiles, TILE, samples), arrived,
        synthesis_table(samples, aper),
    )


def solution(mesh):
    split = P(("sail", "cable"), None)
    return jax.shard_map(
        body,
        mesh=mesh,
        in_specs=(split, split, split, split, split, P(), P()),
        out_specs=split,
        check_vma=False,
    )
```

```python
import math

import jax
import jax.numpy as jnp
import ml_dtypes
import numpy as np
from jax import lax
from jax.experimental import pallas as pl
from jax.experimental.pallas import tpu as pltpu
from jax.sharding import PartitionSpec as P

HALO = 64
DISTINCT = 64
PAD = 8
TILE = 256
STEP = 1024
PITCH = 5
CHUNKS = 8
UNROLL = 8
HEAD = 4
F32 = jnp.float32
BF16 = jnp.bfloat16


def forward_table(samples):
    turns = np.arange(samples)[:, None] * np.arange(samples // 2)[None, :] % samples
    angle = turns * (2.0 * math.pi / samples)
    table = np.concatenate([np.cos(angle), -np.sin(angle)], axis=1) / math.sqrt(samples)
    return jnp.asarray(table.astype(np.float32).astype(ml_dtypes.bfloat16))


def synthesis_table(samples, aperture):
    turns = np.arange(samples // 2)[:, None] * np.arange(samples)[None, :] % samples
    angle = turns * (2.0 * math.pi / samples)
    scale = math.sqrt(aperture * (samples // 2))
    table = np.concatenate([np.cos(angle), -np.sin(angle)], axis=0) / scale
    return jnp.asarray(table.astype(np.float32).astype(ml_dtypes.bfloat16))


def turned(values):
    lines, cap = values.shape
    return jnp.concatenate([values, jnp.zeros((cap - lines, cap), values.dtype)], axis=0).T


def order_kernel(owner_ref, rows_ref, out_ref):
    for g in range(rows_ref.shape[0]):
        out_ref[owner_ref[g]] = rows_ref[g : g + 1, :]


def first_entries(rows):
    lines, cap = rows.shape
    sub = lax.broadcasted_iota(jnp.int32, (cap, cap), 0)
    lane = lax.broadcasted_iota(jnp.int32, (cap, cap), 1)
    earlier = sub < lane
    columns = turned(rows)
    repeats = []
    for g in range(lines):
        same = (columns[:, g : g + 1] == rows[g : g + 1, :]) & earlier
        repeats.append(jnp.max(jnp.where(same, 1.0, 0.0), axis=0, keepdims=True))
    once = 1.0 - jnp.concatenate(repeats, axis=0)
    before = jnp.where(earlier, 1.0, 0.0).astype(BF16)
    place = jnp.dot(once.astype(BF16), before, preferred_element_type=F32)
    return columns, jnp.where(once > 0.0, place, -1.0).astype(jnp.int32)


def put_rows(ref, start, block):
    for q in range(4):
        at = pl.ds(start + q, block.shape[0], stride=PITCH)
        ref[at, :] = block[:, 128 * q : 128 * (q + 1)]


def gather_rows(index, rows_ref, held_ref, out_ref, base, count):
    sub = lax.broadcasted_iota(jnp.int32, (8, 128), 0)
    for k in range(0, count, 2):
        a = rows_ref[pl.ds(index(k) + PAD, 8), :]
        b = rows_ref[pl.ds(index(k + 1) + PAD - 4, 8), :]
        held_ref[pl.ds(pl.multiple_of(base * 4, 8) + 4 * k, 8), :] = jnp.where(sub < 4, a, b)
    for q in range(4):
        part = held_ref[pl.ds(base * 4 + q, count, stride=4), :]
        out_ref[pl.ds(base, count), 128 * q : 128 * (q + 1)] = part.astype(BF16)


def groups(peers):
    sizes = []
    while peers > 2:
        sizes.append(peers // 2)
        peers -= peers // 2
    return sizes + [peers]


def spectra_kernel(
    lists_ref, traces_hbm, table_hbm, first_hbm, last_hbm, out_hbm,
    traces_ref, table_ref, edge_ref, rows_ref, held_ref, out_ref, distinct_ref, asked_ref,
    in_sems, table_sem, asked_sem, edge_sems, out_sems,
):
    parts = len(range(0, traces_ref.shape[0], STEP))
    table = pltpu.make_async_copy(table_hbm, table_ref, table_sem)
    table.start()
    loads = []
    stores = []
    for b in range(parts):
        at = pl.ds(b * STEP, STEP)
        loads.append(pltpu.make_async_copy(traces_hbm.at[at], traces_ref.at[at], in_sems.at[b]))
        loads[b].start()
    lists = lists_ref[...]
    columns, place = first_entries(lists)
    places = turned(place)
    lane = lax.broadcasted_iota(jnp.int32, columns.shape, 1)
    for g in range(lists.shape[0]):
        match = places[:, g : g + 1] == lane
        picked = jnp.max(jnp.where(match, columns[:, g : g + 1], 0), axis=0, keepdims=True)
        distinct_ref[g : g + 1, :] = picked * PITCH
    asking = pltpu.make_async_copy(distinct_ref, asked_ref, asked_sem)
    asking.start()
    table.wait()
    for b in range(parts):
        at = pl.ds(b * STEP, STEP)
        loads[b].wait()
        spectra = jnp.dot(
            traces_ref[at, :], table_ref[...], preferred_element_type=F32
        ).astype(BF16)
        put_rows(rows_ref, PAD + b * STEP * PITCH, spectra.astype(F32))
        for edge, hbm, part, first in ((0, first_hbm, 0, 0), (1, last_hbm, parts - 1, STEP - HALO)):
            if b == part:
                edge_ref[edge] = spectra[first : first + HALO]
                stores.append(pltpu.make_async_copy(edge_ref.at[edge], hbm, edge_sems.at[edge]))
                stores[edge].start()
    asking.wait()
    peers = asked_ref.shape[0]
    sends = []
    done = 0
    for n, each in enumerate(groups(peers)):

        def one(p, _):
            base = pl.multiple_of(p * DISTINCT, DISTINCT)
            gather_rows(lambda k: asked_ref[p, k], rows_ref, held_ref, out_ref, base, DISTINCT)
            return 0

        lax.fori_loop(done, done + each, one, 0)
        at = pl.ds(done * DISTINCT, each * DISTINCT)
        sends.append(pltpu.make_async_copy(out_ref.at[at], out_hbm.at[at], out_sems.at[n]))
        sends[n].start()
        done += each
    for copy in stores + sends:
        copy.wait()


def slots_kernel(
    owner_ref, rows_ref, src_ref, rcv_ref, taper_ref, key_ref, value_ref, rank_ref
):
    lines, cap = rows_ref.shape
    outs = rcv_ref.shape[0]
    rows = rows_ref[...]
    columns, place = first_entries(rows)
    places = turned(place)
    for g in range(lines):
        same = columns[:, g : g + 1] == rows[g : g + 1, :]
        rank_ref[g : g + 1, :] = jnp.max(
            jnp.where(same, places[:, g : g + 1], -1), axis=0, keepdims=True
        )
    line = lax.broadcasted_iota(jnp.int32, (lines, cap), 0)
    first = jnp.zeros((lines, cap), F32)
    for g in range(lines):
        first = jnp.where(line == g, (owner_ref[g] * DISTINCT).astype(F32), first)
    rank = rank_ref[...].astype(F32).astype(BF16)
    sub = lax.broadcasted_iota(jnp.int32, (cap, cap), 0)

    def some(b, _):
        at = pl.multiple_of(b * 8, 8)
        slots = rcv_ref[pl.ds(at, 8), :]
        rows = []
        for u in range(8):
            slot = slots[u : u + 1, :]
            at_slot = (sub == (slot & (cap - 1))).astype(F32).astype(BF16)
            found = jnp.dot(rank, at_slot, preferred_element_type=F32) + first
            rows.append(
                jnp.sum(jnp.where(line == slot // cap, found, 0.0), axis=0, keepdims=True)
            )
        rows = jnp.concatenate(rows, axis=0).astype(jnp.int32)
        out = lax.broadcasted_iota(jnp.int32, (8, cap), 0) + at
        key_ref[pl.ds(at, 8), :] = (rows * outs + out) * 16 + taper_ref[pl.ds(at, 8), :]
        value_ref[pl.ds(at, 8), :] = src_ref[pl.ds(at, 8), :] * PITCH
        return 0

    lax.fori_loop(0, outs // 8, some, 0)


def sources_kernel(
    src_ref, traces_hbm, table_hbm, before_ref, after_ref, out_ref,
    traces_ref, table_ref, all_ref, held_ref, sems,
):
    step = pl.program_id(0)

    @pl.when(step == 0)
    def _():
        own = traces_ref.shape[0]
        copies = [
            pltpu.make_async_copy(traces_hbm, traces_ref, sems.at[0]),
            pltpu.make_async_copy(table_hbm, table_ref, sems.at[1]),
        ]
        for copy in copies:
            copy.start()
        put_rows(all_ref, PAD, before_ref[...].astype(F32))
        put_rows(all_ref, PAD + (HALO + own) * PITCH, after_ref[...].astype(F32))
        for copy in copies:
            copy.wait()

        def one(b, _):
            at = pl.multiple_of(b * STEP, STEP)
            spectra = jnp.dot(
                traces_ref[pl.ds(at, STEP), :], table_ref[...], preferred_element_type=F32
            ).astype(BF16)
            put_rows(all_ref, PAD + (HALO + at) * PITCH, spectra.astype(F32))
            return 0

        lax.fori_loop(0, own // STEP, one, 0)

    def one(c, _):
        base = pl.multiple_of(c * 64, 64)
        first = step * out_ref.shape[0] + base
        gather_rows(lambda k: src_ref[first + k], all_ref, held_ref, out_ref, base, 64)
        return 0

    lax.fori_loop(0, out_ref.shape[0] // 64, one, 0)


def pairs_kernel(
    meet_ref, taper_ref, key_ref, source_hbm, arrived_ref, synth_hbm, out_ref,
    source_ref, synth_ref, sum_ref, weight_ref, hot_ref, product_ref, sems, synth_sem,
):
    tiles, _, samples = source_ref.shape
    outs = out_ref.shape[0]
    half = samples // 2
    last = arrived_ref.shape[0] // TILE - 1
    chunk = tiles // CHUNKS

    def load(c):
        at = pl.ds(c * chunk, chunk)
        return pltpu.make_async_copy(source_hbm.at[at], source_ref.at[at], sems.at[c])

    for c in range(CHUNKS):
        load(c).start()
    synth_copy = pltpu.make_async_copy(synth_hbm, synth_ref, synth_sem)
    synth_copy.start()
    meets = meet_ref.shape[0]
    entry = key_ref[...] & 15
    weights = jnp.zeros(entry.shape, F32)
    for k in range(taper_ref.shape[0]):
        weights = jnp.where(entry == k, taper_ref[k], weights)
    weight_ref[...] = weights
    sum_ref[...] = jnp.zeros_like(sum_ref)
    sub = lax.broadcasted_iota(jnp.int32, (TILE, TILE), 0)
    out = lax.broadcasted_iota(jnp.int32, (outs, TILE), 0)

    def some(base, count):
        for u in range(count):
            meet = meet_ref[base + u]
            t = meet & 63
            b = meet // 64
            at = pl.multiple_of(jnp.minimum(b, last) * TILE, TILE)
            key = key_ref[pl.ds(t, 1), :]
            row = key // (16 * outs)
            here = jnp.where(row // TILE == b, weight_ref[pl.ds(t, 1), :], 0.0)
            spread = jnp.where(out == ((key // 16) & (outs - 1)), here, 0.0).astype(BF16)
            hot = jnp.where(sub == (row & (TILE - 1)), 1.0, 0.0).astype(BF16)
            right = lax.dot_general(
                hot, arrived_ref[pl.ds(at, TILE), :], (((0,), (0,)), ((), ())),
                preferred_element_type=F32,
            ).astype(BF16)
            left = source_ref[t]
            sr, si, rr, ri = left[:, :half], left[:, half:], right[:, :half], right[:, half:]
            product = jnp.concatenate([sr * rr - si * ri, sr * ri + si * rr], axis=1)
            product_ref[u * TILE : (u + 1) * TILE, :] = product
            hot_ref[:, u * TILE : (u + 1) * TILE] = spread
        width = count * TILE
        sum_ref[...] += jnp.dot(
            hot_ref[:, :width], product_ref[:width, :], preferred_element_type=F32
        )

    load(0).wait()
    some(0, HEAD)

    def later(c, _):
        base = HEAD + c * UNROLL

        @pl.when(base < tiles)
        def _():
            for u in range(UNROLL // chunk):
                part = base // chunk + u

                @pl.when(part < CHUNKS)
                def _():
                    load(part).wait()

        some(base, UNROLL)
        return 0

    rest = (meets - HEAD) % UNROLL
    lax.fori_loop(0, (meets - HEAD) // UNROLL, later, 0)
    if rest:
        some(meets - rest, rest)
    synth_copy.wait()
    summed = sum_ref[...].astype(BF16)
    out_ref[...] = jnp.dot(summed, synth_ref[...], preferred_element_type=F32).astype(BF16)


def meet_list(ends, meets):
    tiles = ends.shape[1]
    counts = ends[1] - ends[0] + 1
    tile = jnp.arange(tiles, dtype=jnp.int32)
    ahead = jnp.sum(jnp.where(tile[None, :] < tile[:, None], counts[None, :], 0), axis=1)
    place = jnp.arange(meets, dtype=jnp.int32)[:, None]
    inside = (place >= ahead[None, :]) & (place < (ahead + counts)[None, :])
    value = (ends[0] + place - ahead[None, :]) * 64 + tile[None, :]
    listed = jnp.sum(jnp.where(inside, value, 0), axis=1)
    used = jnp.any(inside, axis=1)
    return jnp.where(used, listed, (meets - tiles) * 64 + tiles - 1).astype(jnp.int32)


VMEM = pl.BlockSpec(memory_space=pltpu.VMEM)
SMEM = pl.BlockSpec(memory_space=pltpu.SMEM)
HBM = pl.BlockSpec(memory_space=pltpu.HBM)


def shape(dims, kind):
    return jax.ShapeDtypeStruct(dims, kind)


def params(mib):
    return pltpu.CompilerParams(vmem_limit_bytes=mib << 20)


def cost(flops, moved):
    return pl.CostEstimate(flops=flops, bytes_accessed=moved, transcendentals=0)


def body(traces, src_index, rcv_index, taper_index, fetch_rows, line_owner, taper_table):
    sails = lax.axis_size("sail")
    cables = lax.axis_size("cable")
    tr_rows, samples = traces.shape
    outs, aper = src_index.shape
    cap = fetch_rows.shape[1]
    lists = pl.pallas_call(
        order_kernel,
        in_specs=[SMEM, VMEM],
        out_specs=VMEM,
        out_shape=shape((sails, 1, cap), jnp.int32),
        compiler_params=params(56),
        name="order",
    )(line_owner, fetch_rows)
    lists = lax.all_to_all(lists, "sail", split_axis=0, concat_axis=0, tiled=True)
    fetched = sails * DISTINCT
    parts = tr_rows // STEP
    table = forward_table(samples)
    first, last, outgoing = pl.pallas_call(
        spectra_kernel,
        in_specs=[VMEM, HBM, HBM],
        out_specs=[HBM, HBM, HBM],
        out_shape=[
            shape((HALO, samples), BF16),
            shape((HALO, samples), BF16),
            shape((fetched, samples), BF16),
        ],
        scratch_shapes=[
            pltpu.VMEM((tr_rows, samples), BF16),
            pltpu.VMEM((samples, samples), BF16),
            pltpu.VMEM((2, HALO, samples), BF16),
            pltpu.VMEM((tr_rows * PITCH + 2 * PAD, 128), F32),
            pltpu.VMEM((fetched * 4 + PAD, 128), F32),
            pltpu.VMEM((fetched, samples), BF16),
            pltpu.VMEM((sails, cap), jnp.int32),
            pltpu.SMEM((sails, cap), jnp.int32),
            pltpu.SemaphoreType.DMA((parts,)),
            pltpu.SemaphoreType.DMA,
            pltpu.SemaphoreType.DMA,
            pltpu.SemaphoreType.DMA((2,)),
            pltpu.SemaphoreType.DMA((len(groups(sails)),)),
        ],
        compiler_params=params(56),
        name="spectra",
    )(lists.reshape(sails, cap), traces, table)
    arrived = lax.all_to_all(
        outgoing.reshape(sails, DISTINCT, samples), "sail", split_axis=0, concat_axis=0, tiled=True
    ).reshape(fetched, samples)
    up = [(i, i + 1) for i in range(cables - 1)]
    before = lax.ppermute(last, "cable", up)
    after = lax.ppermute(first, "cable", [(j, i) for i, j in up])
    key, value = pl.pallas_call(
        slots_kernel,
        in_specs=[SMEM] + [VMEM] * 4,
        out_specs=[VMEM, VMEM],
        out_shape=[shape((outs, aper), jnp.int32)] * 2,
        scratch_shapes=[pltpu.VMEM((sails, cap), jnp.int32)],
        compiler_params=params(56),
        name="slots",
        cost_estimate=cost(0, 10 << 20),
    )(line_owner, fetch_rows, src_index, rcv_index, taper_index)
    count = outs * aper
    key, value = lax.sort((key.reshape(-1), value.reshape(-1)), num_keys=1, is_stable=False)
    tiles = count // TILE
    blocks = fetched // TILE
    ends = key.reshape(tiles, TILE)[:, :: TILE - 1].T // (16 * outs * TILE)
    meets = -(-(tiles + blocks) // HEAD) * HEAD
    sources = pl.pallas_call(
        sources_kernel,
        grid=(8,),
        in_specs=[SMEM, HBM, HBM, VMEM, VMEM],
        out_specs=pl.BlockSpec((count // 8, samples), lambda b: (b, 0)),
        out_shape=shape((count, samples), BF16),
        scratch_shapes=[
            pltpu.VMEM((tr_rows, samples), BF16),
            pltpu.VMEM((samples, samples), BF16),
            pltpu.VMEM(((tr_rows + 2 * HALO) * PITCH + 2 * PAD, 128), F32),
            pltpu.VMEM((count // 8 * 4 + PAD, 128), F32),
            pltpu.SemaphoreType.DMA((2,)),
        ],
        compiler_params=params(56),
        name="sources",
        cost_estimate=cost(0, 40 << 20),
    )(value, traces, table, before, after)
    return pl.pallas_call(
        pairs_kernel,
        in_specs=[SMEM, SMEM, VMEM, HBM, VMEM, HBM],
        out_specs=VMEM,
        out_shape=shape((outs, samples), BF16),
        scratch_shapes=[
            pltpu.VMEM((tiles, TILE, samples), BF16),
            pltpu.VMEM((samples, samples), BF16),
            pltpu.VMEM((outs, samples), F32),
            pltpu.VMEM((tiles, TILE), F32),
            pltpu.VMEM((outs, UNROLL * TILE), BF16),
            pltpu.VMEM((UNROLL * TILE, samples), BF16),
            pltpu.SemaphoreType.DMA((CHUNKS,)),
            pltpu.SemaphoreType.DMA,
        ],
        compiler_params=params(50),
        name="pairs",
    )(
        meet_list(ends, meets), taper_table, key.reshape(tiles, TILE), sources.reshape(tiles, TILE, samples), arrived,
        synthesis_table(samples, aper),
    )


def solution(mesh):
    split = P(("sail", "cable"), None)
    return jax.shard_map(
        body,
        mesh=mesh,
        in_specs=(split, split, split, split, split, P(), P()),
        out_specs=split,
        check_vma=False,
    )
```

```python
import math

import jax
import jax.numpy as jnp
import ml_dtypes
import numpy as np
from jax import lax
from jax.experimental import pallas as pl
from jax.experimental.pallas import tpu as pltpu
from jax.sharding import PartitionSpec as P

HALO = 64
DISTINCT = 64
PAD = 8
TILE = 256
STEP = 1024
PITCH = 5
CHUNKS = 8
UNROLL = 8
HEAD = 4
F32 = jnp.float32
BF16 = jnp.bfloat16


def forward_table(samples):
    turns = np.arange(samples)[:, None] * np.arange(samples // 2)[None, :] % samples
    angle = turns * (2.0 * math.pi / samples)
    table = np.concatenate([np.cos(angle), -np.sin(angle)], axis=1) / math.sqrt(samples)
    return jnp.asarray(table.astype(np.float32).astype(ml_dtypes.bfloat16))


def synthesis_table(samples, aperture):
    turns = np.arange(samples // 2)[:, None] * np.arange(samples)[None, :] % samples
    angle = turns * (2.0 * math.pi / samples)
    scale = math.sqrt(aperture * (samples // 2))
    table = np.concatenate([np.cos(angle), -np.sin(angle)], axis=0) / scale
    return jnp.asarray(table.astype(np.float32).astype(ml_dtypes.bfloat16))


def turned(values):
    lines, cap = values.shape
    return jnp.concatenate([values, jnp.zeros((cap - lines, cap), values.dtype)], axis=0).T


def order_kernel(owner_ref, rows_ref, out_ref):
    for g in range(rows_ref.shape[0]):
        out_ref[owner_ref[g]] = rows_ref[g : g + 1, :]


def first_entries(rows):
    lines, cap = rows.shape
    sub = lax.broadcasted_iota(jnp.int32, (cap, cap), 0)
    lane = lax.broadcasted_iota(jnp.int32, (cap, cap), 1)
    earlier = sub < lane
    columns = turned(rows)
    repeats = []
    for g in range(lines):
        same = (columns[:, g : g + 1] == rows[g : g + 1, :]) & earlier
        repeats.append(jnp.max(jnp.where(same, 1.0, 0.0), axis=0, keepdims=True))
    once = 1.0 - jnp.concatenate(repeats, axis=0)
    before = jnp.where(earlier, 1.0, 0.0).astype(BF16)
    place = jnp.dot(once.astype(BF16), before, preferred_element_type=F32)
    return columns, jnp.where(once > 0.0, place, -1.0).astype(jnp.int32)


def put_rows(ref, start, block):
    for q in range(4):
        at = pl.ds(start + q, block.shape[0], stride=PITCH)
        ref[at, :] = block[:, 128 * q : 128 * (q + 1)]


def gather_rows(index, rows_ref, held_ref, out_ref, base, count):
    sub = lax.broadcasted_iota(jnp.int32, (8, 128), 0)
    for k in range(0, count, 2):
        a = rows_ref[pl.ds(index(k) + PAD, 8), :]
        b = rows_ref[pl.ds(index(k + 1) + PAD - 4, 8), :]
        held_ref[pl.ds(pl.multiple_of(base * 4, 8) + 4 * k, 8), :] = jnp.where(sub < 4, a, b)
    for q in range(4):
        part = held_ref[pl.ds(base * 4 + q, count, stride=4), :]
        out_ref[pl.ds(base, count), 128 * q : 128 * (q + 1)] = part.astype(BF16)


def groups(peers):
    sizes = []
    while peers > 2:
        sizes.append(peers // 2)
        peers -= peers // 2
    return sizes + [peers]


def spectra_kernel(
    lists_hbm, traces_hbm, table_hbm, first_hbm, last_hbm, out_hbm,
    traces_ref, table_ref, edge_ref, rows_ref, held_ref, out_ref, lists_ref, distinct_ref, asked_ref,
    in_sems, table_sem, lists_sem, asked_sem, edge_sems, out_sems,
):
    parts = len(range(0, traces_ref.shape[0], STEP))
    listing = pltpu.make_async_copy(lists_hbm, lists_ref, lists_sem)
    listing.start()
    table = pltpu.make_async_copy(table_hbm, table_ref, table_sem)
    table.start()
    loads = []
    stores = []
    for b in range(parts):
        at = pl.ds(b * STEP, STEP)
        loads.append(pltpu.make_async_copy(traces_hbm.at[at], traces_ref.at[at], in_sems.at[b]))
        loads[b].start()
    listing.wait()
    lists = lists_ref[...]
    columns, place = first_entries(lists)
    places = turned(place)
    lane = lax.broadcasted_iota(jnp.int32, columns.shape, 1)
    for g in range(lists.shape[0]):
        match = places[:, g : g + 1] == lane
        picked = jnp.max(jnp.where(match, columns[:, g : g + 1], 0), axis=0, keepdims=True)
        distinct_ref[g : g + 1, :] = picked * PITCH
    asking = pltpu.make_async_copy(distinct_ref, asked_ref, asked_sem)
    asking.start()
    table.wait()
    for b in range(parts):
        at = pl.ds(b * STEP, STEP)
        loads[b].wait()
        spectra = jnp.dot(
            traces_ref[at, :], table_ref[...], preferred_element_type=F32
        ).astype(BF16)
        put_rows(rows_ref, PAD + b * STEP * PITCH, spectra.astype(F32))
        for edge, hbm, part, first in ((0, first_hbm, 0, 0), (1, last_hbm, parts - 1, STEP - HALO)):
            if b == part:
                edge_ref[edge] = spectra[first : first + HALO]
                stores.append(pltpu.make_async_copy(edge_ref.at[edge], hbm, edge_sems.at[edge]))
                stores[edge].start()
    asking.wait()
    peers = asked_ref.shape[0]
    sends = []
    done = 0
    for n, each in enumerate(groups(peers)):

        def one(p, _):
            base = pl.multiple_of(p * DISTINCT, DISTINCT)
            gather_rows(lambda k: asked_ref[p, k], rows_ref, held_ref, out_ref, base, DISTINCT)
            return 0

        lax.fori_loop(done, done + each, one, 0)
        at = pl.ds(done * DISTINCT, each * DISTINCT)
        sends.append(pltpu.make_async_copy(out_ref.at[at], out_hbm.at[at], out_sems.at[n]))
        sends[n].start()
        done += each
    for copy in stores + sends:
        copy.wait()


def slots_kernel(
    owner_ref, rows_ref, src_ref, rcv_ref, taper_ref, key_ref, value_ref, rank_ref
):
    lines, cap = rows_ref.shape
    outs = rcv_ref.shape[0]
    rows = rows_ref[...]
    columns, place = first_entries(rows)
    places = turned(place)
    for g in range(lines):
        same = columns[:, g : g + 1] == rows[g : g + 1, :]
        rank_ref[g : g + 1, :] = jnp.max(
            jnp.where(same, places[:, g : g + 1], -1), axis=0, keepdims=True
        )
    line = lax.broadcasted_iota(jnp.int32, (lines, cap), 0)
    first = jnp.zeros((lines, cap), F32)
    for g in range(lines):
        first = jnp.where(line == g, (owner_ref[g] * DISTINCT).astype(F32), first)
    rank = rank_ref[...].astype(F32).astype(BF16)
    sub = lax.broadcasted_iota(jnp.int32, (cap, cap), 0)

    def some(b, _):
        at = pl.multiple_of(b * 8, 8)
        slots = rcv_ref[pl.ds(at, 8), :]
        rows = []
        for u in range(8):
            slot = slots[u : u + 1, :]
            at_slot = (sub == (slot & (cap - 1))).astype(F32).astype(BF16)
            found = jnp.dot(rank, at_slot, preferred_element_type=F32) + first
            rows.append(
                jnp.sum(jnp.where(line == slot // cap, found, 0.0), axis=0, keepdims=True)
            )
        rows = jnp.concatenate(rows, axis=0).astype(jnp.int32)
        out = lax.broadcasted_iota(jnp.int32, (8, cap), 0) + at
        key_ref[pl.ds(at, 8), :] = (rows * outs + out) * 16 + taper_ref[pl.ds(at, 8), :]
        value_ref[pl.ds(at, 8), :] = src_ref[pl.ds(at, 8), :] * PITCH
        return 0

    lax.fori_loop(0, outs // 8, some, 0)


def sources_kernel(
    src_ref, traces_hbm, table_hbm, before_ref, after_ref, out_ref,
    traces_ref, table_ref, all_ref, held_ref, sems,
):
    step = pl.program_id(0)

    @pl.when(step == 0)
    def _():
        own = traces_ref.shape[0]
        copies = [
            pltpu.make_async_copy(traces_hbm, traces_ref, sems.at[0]),
            pltpu.make_async_copy(table_hbm, table_ref, sems.at[1]),
        ]
        for copy in copies:
            copy.start()
        put_rows(all_ref, PAD, before_ref[...].astype(F32))
        put_rows(all_ref, PAD + (HALO + own) * PITCH, after_ref[...].astype(F32))
        for copy in copies:
            copy.wait()

        def one(b, _):
            at = pl.multiple_of(b * STEP, STEP)
            spectra = jnp.dot(
                traces_ref[pl.ds(at, STEP), :], table_ref[...], preferred_element_type=F32
            ).astype(BF16)
            put_rows(all_ref, PAD + (HALO + at) * PITCH, spectra.astype(F32))
            return 0

        lax.fori_loop(0, own // STEP, one, 0)

    def one(c, _):
        base = pl.multiple_of(c * 64, 64)
        first = step * out_ref.shape[0] + base
        gather_rows(lambda k: src_ref[first + k], all_ref, held_ref, out_ref, base, 64)
        return 0

    lax.fori_loop(0, out_ref.shape[0] // 64, one, 0)


def pairs_kernel(
    meet_ref, taper_ref, key_ref, source_hbm, arrived_ref, synth_hbm, out_ref,
    source_ref, synth_ref, sum_ref, weight_ref, hot_ref, product_ref, sems, synth_sem,
):
    tiles, _, samples = source_ref.shape
    outs = out_ref.shape[0]
    half = samples // 2
    last = arrived_ref.shape[0] // TILE - 1
    chunk = tiles // CHUNKS

    def load(c):
        at = pl.ds(c * chunk, chunk)
        return pltpu.make_async_copy(source_hbm.at[at], source_ref.at[at], sems.at[c])

    for c in range(CHUNKS):
        load(c).start()
    synth_copy = pltpu.make_async_copy(synth_hbm, synth_ref, synth_sem)
    synth_copy.start()
    meets = meet_ref.shape[0]
    entry = key_ref[...] & 15
    weights = jnp.zeros(entry.shape, F32)
    for k in range(taper_ref.shape[0]):
        weights = jnp.where(entry == k, taper_ref[k], weights)
    weight_ref[...] = weights
    sum_ref[...] = jnp.zeros_like(sum_ref)
    sub = lax.broadcasted_iota(jnp.int32, (TILE, TILE), 0)
    out = lax.broadcasted_iota(jnp.int32, (outs, TILE), 0)

    def some(base, count):
        for u in range(count):
            meet = meet_ref[base + u]
            t = meet & 63
            b = meet // 64
            at = pl.multiple_of(jnp.minimum(b, last) * TILE, TILE)
            key = key_ref[pl.ds(t, 1), :]
            row = key // (16 * outs)
            here = jnp.where(row // TILE == b, weight_ref[pl.ds(t, 1), :], 0.0)
            spread = jnp.where(out == ((key // 16) & (outs - 1)), here, 0.0).astype(BF16)
            hot = jnp.where(sub == (row & (TILE - 1)), 1.0, 0.0).astype(BF16)
            right = lax.dot_general(
                hot, arrived_ref[pl.ds(at, TILE), :], (((0,), (0,)), ((), ())),
                preferred_element_type=F32,
            ).astype(BF16)
            left = source_ref[t]
            sr, si, rr, ri = left[:, :half], left[:, half:], right[:, :half], right[:, half:]
            product = jnp.concatenate([sr * rr - si * ri, sr * ri + si * rr], axis=1)
            product_ref[u * TILE : (u + 1) * TILE, :] = product
            hot_ref[:, u * TILE : (u + 1) * TILE] = spread
        width = count * TILE
        sum_ref[...] += jnp.dot(
            hot_ref[:, :width], product_ref[:width, :], preferred_element_type=F32
        )

    load(0).wait()
    some(0, HEAD)

    def later(c, _):
        base = HEAD + c * UNROLL

        @pl.when(base < tiles)
        def _():
            for u in range(UNROLL // chunk):
                part = base // chunk + u

                @pl.when(part < CHUNKS)
                def _():
                    load(part).wait()

        some(base, UNROLL)
        return 0

    rest = (meets - HEAD) % UNROLL
    lax.fori_loop(0, (meets - HEAD) // UNROLL, later, 0)
    if rest:
        some(meets - rest, rest)
    synth_copy.wait()
    summed = sum_ref[...].astype(BF16)
    out_ref[...] = jnp.dot(summed, synth_ref[...], preferred_element_type=F32).astype(BF16)


def meet_list(ends, meets):
    tiles = ends.shape[1]
    counts = ends[1] - ends[0] + 1
    tile = jnp.arange(tiles, dtype=jnp.int32)
    ahead = jnp.sum(jnp.where(tile[None, :] < tile[:, None], counts[None, :], 0), axis=1)
    place = jnp.arange(meets, dtype=jnp.int32)[:, None]
    inside = (place >= ahead[None, :]) & (place < (ahead + counts)[None, :])
    value = (ends[0] + place - ahead[None, :]) * 64 + tile[None, :]
    listed = jnp.sum(jnp.where(inside, value, 0), axis=1)
    used = jnp.any(inside, axis=1)
    return jnp.where(used, listed, (meets - tiles) * 64 + tiles - 1).astype(jnp.int32)


VMEM = pl.BlockSpec(memory_space=pltpu.VMEM)
SMEM = pl.BlockSpec(memory_space=pltpu.SMEM)
HBM = pl.BlockSpec(memory_space=pltpu.HBM)


def shape(dims, kind):
    return jax.ShapeDtypeStruct(dims, kind)


def params(mib):
    return pltpu.CompilerParams(vmem_limit_bytes=mib << 20)


def cost(flops, moved):
    return pl.CostEstimate(flops=flops, bytes_accessed=moved, transcendentals=0)


def body(traces, src_index, rcv_index, taper_index, fetch_rows, line_owner, taper_table):
    sails = lax.axis_size("sail")
    cables = lax.axis_size("cable")
    tr_rows, samples = traces.shape
    outs, aper = src_index.shape
    cap = fetch_rows.shape[1]
    lists = pl.pallas_call(
        order_kernel,
        in_specs=[SMEM, VMEM],
        out_specs=VMEM,
        out_shape=shape((sails, 1, cap), jnp.int32),
        compiler_params=params(56),
        name="order",
    )(line_owner, fetch_rows)
    lists = lax.all_to_all(lists, "sail", split_axis=0, concat_axis=0, tiled=True)
    fetched = sails * DISTINCT
    parts = tr_rows // STEP
    table = forward_table(samples)
    first, last, outgoing = pl.pallas_call(
        spectra_kernel,
        in_specs=[HBM, HBM, HBM],
        out_specs=[HBM, HBM, HBM],
        out_shape=[
            shape((HALO, samples), BF16),
            shape((HALO, samples), BF16),
            shape((fetched, samples), BF16),
        ],
        scratch_shapes=[
            pltpu.VMEM((tr_rows, samples), BF16),
            pltpu.VMEM((samples, samples), BF16),
            pltpu.VMEM((2, HALO, samples), BF16),
            pltpu.VMEM((tr_rows * PITCH + 2 * PAD, 128), F32),
            pltpu.VMEM((fetched * 4 + PAD, 128), F32),
            pltpu.VMEM((fetched, samples), BF16),
            pltpu.VMEM((sails, cap), jnp.int32),
            pltpu.VMEM((sails, cap), jnp.int32),
            pltpu.SMEM((sails, cap), jnp.int32),
            pltpu.SemaphoreType.DMA((parts,)),
            pltpu.SemaphoreType.DMA,
            pltpu.SemaphoreType.DMA,
            pltpu.SemaphoreType.DMA,
            pltpu.SemaphoreType.DMA((2,)),
            pltpu.SemaphoreType.DMA((len(groups(sails)),)),
        ],
        compiler_params=params(56),
        name="spectra",
    )(lists.reshape(sails, cap), traces, table)
    arrived = lax.all_to_all(
        outgoing.reshape(sails, DISTINCT, samples), "sail", split_axis=0, concat_axis=0, tiled=True
    ).reshape(fetched, samples)
    up = [(i, i + 1) for i in range(cables - 1)]
    before = lax.ppermute(last, "cable", up)
    after = lax.ppermute(first, "cable", [(j, i) for i, j in up])
    key, value = pl.pallas_call(
        slots_kernel,
        in_specs=[SMEM] + [VMEM] * 4,
        out_specs=[VMEM, VMEM],
        out_shape=[shape((outs, aper), jnp.int32)] * 2,
        scratch_shapes=[pltpu.VMEM((sails, cap), jnp.int32)],
        compiler_params=params(56),
        name="slots",
        cost_estimate=cost(0, 10 << 20),
    )(line_owner, fetch_rows, src_index, rcv_index, taper_index)
    count = outs * aper
    key, value = lax.sort((key.reshape(-1), value.reshape(-1)), num_keys=1, is_stable=False)
    tiles = count // TILE
    blocks = fetched // TILE
    ends = key.reshape(tiles, TILE)[:, :: TILE - 1].T // (16 * outs * TILE)
    meets = -(-(tiles + blocks) // HEAD) * HEAD
    sources = pl.pallas_call(
        sources_kernel,
        grid=(8,),
        in_specs=[SMEM, HBM, HBM, VMEM, VMEM],
        out_specs=pl.BlockSpec((count // 8, samples), lambda b: (b, 0)),
        out_shape=shape((count, samples), BF16),
        scratch_shapes=[
            pltpu.VMEM((tr_rows, samples), BF16),
            pltpu.VMEM((samples, samples), BF16),
            pltpu.VMEM(((tr_rows + 2 * HALO) * PITCH + 2 * PAD, 128), F32),
            pltpu.VMEM((count // 8 * 4 + PAD, 128), F32),
            pltpu.SemaphoreType.DMA((2,)),
        ],
        compiler_params=params(56),
        name="sources",
        cost_estimate=cost(0, 40 << 20),
    )(value, traces, table, before, after)
    return pl.pallas_call(
        pairs_kernel,
        in_specs=[SMEM, SMEM, VMEM, HBM, VMEM, HBM],
        out_specs=VMEM,
        out_shape=shape((outs, samples), BF16),
        scratch_shapes=[
            pltpu.VMEM((tiles, TILE, samples), BF16),
            pltpu.VMEM((samples, samples), BF16),
            pltpu.VMEM((outs, samples), F32),
            pltpu.VMEM((tiles, TILE), F32),
            pltpu.VMEM((outs, UNROLL * TILE), BF16),
            pltpu.VMEM((UNROLL * TILE, samples), BF16),
            pltpu.SemaphoreType.DMA((CHUNKS,)),
            pltpu.SemaphoreType.DMA,
        ],
        compiler_params=params(50),
        name="pairs",
    )(
        meet_list(ends, meets), taper_table, key.reshape(tiles, TILE), sources.reshape(tiles, TILE, samples), arrived,
        synthesis_table(samples, aper),
    )


def solution(mesh):
    split = P(("sail", "cable"), None)
    return jax.shard_map(
        body,
        mesh=mesh,
        in_specs=(split, split, split, split, split, P(), P()),
        out_specs=split,
        check_vma=False,
    )
```
